768 devices in a mesh: dp: 768 (over y, z, x, core).
Axes of the slice: x: 4, y: 8, z: 12, core: 2. Of those that a mesh axis runs over, the one named last changes fastest.
Arguments:
- query_hidden: bfloat16 [98304, 3584], P('dp'), may hold values from -6 to 6, as said below
- doc_hidden: bfloat16 [98304, 3584], P('dp'), may hold values from -6 to 6, as said below
- gain: float32 [3584], replicated, may hold values from 0.5 to 1.5
- positives: int32 [98304], P('dp'), may hold values from 0 to 127
- neg_blocks: int32 [768, 4], P('dp'), may hold values from 0 to 767, as said below
Outputs:
- mean_loss: float32 [], replicated
- grad_gain: float32 [3584], replicated
- grad_query: bfloat16 [98304, 3584], P('dp')
- grad_doc: bfloat16 [98304, 3584], P('dp')
The draws below stay inside these ranges and needn't reach their ends.
Inputs may be any that keep to these rules, and one draw needn't show every extreme that they name: `neg_blocks`: row b lists 4 block ids; each entry is either b itself (an unused entry) or (b + o) mod 768 with 1 <= |o| <= 2; the entries other than b are distinct, at least one per row, and some row lists all 4 of them. `query_hidden`: rows are pooled hidden states of order one. `doc_hidden`: rows are pooled hidden states of order one.
All inputs are finite; a program needn't handle non-finite values.
Results may differ from the reference program's by a relative error of at most 0.0079.
Values may be sent and summed in bfloat16 or wider, within the bound.
No kernel may reach another device: no remote copies, remote signals or barrier semaphores. Data moves between devices by JAX's collectives and lax.ppermute only.
A program may use at most 64 MiB of HBM per device.

```python
import math
import jax
import jax.numpy as jnp
from jax import lax

D = 3584
BLOCK = 128
RADIUS = 2
TOTAL = 98304
N_DP = 768


def draw_doc_hidden(key, part):
    values = jnp.clip(jax.random.normal(jax.random.fold_in(key, 25), (TOTAL, D), jnp.float32), -6.0, 6.0)
    return values.astype(jnp.bfloat16)


def draw_query_hidden(key, part):
    values = jnp.clip(jax.random.normal(jax.random.fold_in(key, 35), (TOTAL, D), jnp.float32), -6.0, 6.0)
    return values.astype(jnp.bfloat16)


def draw_neg_blocks(key, part):
    blocks = TOTAL // BLOCK
    width = 2 * RADIUS
    offs = jnp.array([o for o in range(-RADIUS, RADIUS + 1) if o != 0], jnp.int32)
    ranks = jax.random.randint(jax.random.fold_in(key, 41), (blocks, width), 0, 1024) * width + jnp.arange(width, dtype=jnp.int32)[None, :]
    order = jnp.argsort(ranks, axis=1, stable=True)
    heavy = jax.random.randint(jax.random.fold_in(key, 42), (blocks,), 0, 4) == 0
    light = jax.random.randint(jax.random.fold_in(key, 43), (blocks,), 1, 3)
    counts = jnp.where(heavy, width, jnp.minimum(light, width)).astype(jnp.int32)
    counts = counts.at[0].set(width)
    chosen = offs[order]
    rows = jnp.arange(blocks, dtype=jnp.int32)[:, None]
    slots = jnp.arange(width, dtype=jnp.int32)[None, :]
    ids = jnp.where(slots < counts[:, None], (rows + chosen) % blocks, rows)
    return ids.astype(jnp.int32)


def with_ends(values, rng, low, top_value):
    index_at = [jax.random.randint(jax.random.fold_in(rng, axis), (), 0, length) for axis, length in enumerate(values.shape)]
    widest = values.shape.index(max(values.shape))
    next_to = index_at[:widest] + [(index_at[widest] + 1) % values.shape[widest]] + index_at[widest + 1:]
    return values.at[tuple(index_at)].set(low).at[tuple(next_to)].set(top_value)


def setup_inputs(seed: int = 0) -> dict:
    key_of = jax.random.split(jax.random.key(seed), 6)
    return {
        "query_hidden": draw_query_hidden(jax.random.fold_in(key_of[5], 71), 0),
        "doc_hidden": draw_doc_hidden(jax.random.fold_in(key_of[5], 71), 0),
        "gain": jnp.clip(1.0 + 0.1 * jax.random.normal(key_of[2], (D,), jnp.float32), 0.5, 1.5),
        "positives": with_ends(jax.random.randint(key_of[3], (TOTAL,), 0, BLOCK), jax.random.fold_in(key_of[3], 1), 0, BLOCK - 1).astype(jnp.int32),
        "neg_blocks": draw_neg_blocks(jax.random.fold_in(key_of[5], 71), 0),
    }


logit_scale = 4.0

def head(hidden, gain):
    values = hidden.astype(jnp.float32)
    factor = lax.rsqrt(lax.optimization_barrier(jnp.mean(values * values, axis=-1, keepdims=True)) + 1e-06)
    return values * factor * gain

def rounded(term):
    held = lax.optimization_barrier(term.astype(jnp.bfloat16))
    return held.astype(jnp.float32)

def reference(query_hidden, doc_hidden, gain, positives, neg_blocks):
    blocks = N_DP
    factor = logit_scale / math.sqrt(D)
    q_norm = head(query_hidden, gain).astype(jnp.bfloat16).reshape(blocks, BLOCK, D)
    d_norm = head(doc_hidden, gain).astype(jnp.bfloat16).reshape(blocks, BLOCK, D)
    pos_blocks = positives.reshape(blocks, BLOCK)
    offsets = [o for o in range(-RADIUS, RADIUS + 1) if o != 0]
    offs = jnp.array(offsets, jnp.int32)
    ids = (jnp.arange(blocks, dtype=jnp.int32)[:, None] + offs[None, :]) % blocks
    flags = jnp.any(neg_blocks[:, None, :] == ids[:, :, None], axis=-1)
    slots = jnp.arange(BLOCK, dtype=jnp.int32)

    def first_pass(index):
        query = q_norm[index]
        onehot = (slots[None, :] == pos_blocks[index][:, None]).astype(jnp.float32)
        own = factor * jnp.dot(query, d_norm[index].T, preferred_element_type=jnp.float32)
        scores = []
        for k, o in enumerate(offsets):
            other = d_norm[(index + o) % blocks]
            scores.append(factor * jnp.dot(query, other.T, preferred_element_type=jnp.float32))
        top = lax.optimization_barrier(jnp.max(own, axis=1))
        for k in range(len(offsets)):
            top = jnp.maximum(top, jnp.where(flags[index, k], lax.optimization_barrier(jnp.max(scores[k], axis=1)), -jnp.inf))
        total = lax.optimization_barrier(jnp.sum(jnp.exp(own - top[:, None]), axis=1))
        for k in range(len(offsets)):
            total = total + jnp.where(flags[index, k], lax.optimization_barrier(jnp.sum(jnp.exp(scores[k] - top[:, None]), axis=1)), 0.0)
        lse = top + jnp.log(total)
        loss = lse - lax.optimization_barrier(jnp.sum(own * onehot, axis=1))
        weight = (jnp.exp(own - lse[:, None]) - onehot).astype(jnp.bfloat16)
        q_grad = rounded(jnp.dot(weight, d_norm[index], preferred_element_type=jnp.float32))
        for k, o in enumerate(offsets):
            other = d_norm[(index + o) % blocks]
            probs = jnp.where(flags[index, k], jnp.exp(scores[k] - lse[:, None]), 0.0).astype(jnp.bfloat16)
            q_grad = q_grad + rounded(jnp.dot(probs, other, preferred_element_type=jnp.float32))
        return (loss, lse, factor * q_grad)
    losses, lses, q_grads = lax.map(first_pass, jnp.arange(blocks, dtype=jnp.int32))

    def second_pass(index):
        docs = d_norm[index]
        onehot = (slots[None, :] == pos_blocks[index][:, None]).astype(jnp.float32)
        own = factor * jnp.dot(q_norm[index], docs.T, preferred_element_type=jnp.float32)
        weight = (jnp.exp(own - lses[index][:, None]) - onehot).astype(jnp.bfloat16)
        d_grad = rounded(jnp.dot(weight.T, q_norm[index], preferred_element_type=jnp.float32))
        for k, o in enumerate(offsets):
            source = (index - o) % blocks
            query = q_norm[source]
            scores = factor * jnp.dot(query, docs.T, preferred_element_type=jnp.float32)
            probs = jnp.where(flags[source, k], jnp.exp(scores - lses[source][:, None]), 0.0).astype(jnp.bfloat16)
            d_grad = d_grad + rounded(jnp.dot(probs.T, query, preferred_element_type=jnp.float32))
        return factor * d_grad
    d_grads = lax.map(second_pass, jnp.arange(blocks, dtype=jnp.int32))
    _, pull_query = jax.vjp(head, query_hidden, gain)
    grad_query, gain_query = pull_query(q_grads.reshape(TOTAL, D))
    _, pull_doc = jax.vjp(head, doc_hidden, gain)
    grad_doc, gain_doc = pull_doc(d_grads.reshape(TOTAL, D))
    mean_loss = jnp.sum(losses) / TOTAL
    grad_gain = (gain_query + gain_doc) / TOTAL
    return (mean_loss, grad_gain, grad_query.astype(jnp.bfloat16), grad_doc.astype(jnp.bfloat16))
```

```python
import functools
import math

import jax
import jax.numpy as jnp
import numpy as np
from jax import lax
from jax.experimental import pallas as pl
from jax.experimental.pallas import tpu as pltpu
from jax.sharding import Mesh
from jax.sharding import PartitionSpec as P

logit_scale = 4.0
ROWS = 128
WIDTH = 3584
FACTOR = logit_scale / math.sqrt(WIDTH)
LANES = 128
GAIN_ROWS = WIDTH // LANES
SUM_ROWS = 32
CHUNK = 512
HIDDEN = -1e30
STEP = 16
f32, bf16 = jnp.float32, jnp.bfloat16
AXES = ("y", "z", "row")

in_vmem = pl.BlockSpec(memory_space=pltpu.VMEM)
anywhere = pl.BlockSpec(memory_space=pl.ANY)
in_smem = pl.BlockSpec(memory_space=pltpu.SMEM)


def held(shape, dtype):
    return pltpu.VMEM(shape, dtype)


def call(kernel, out_shape, args, scratch=(), aliases=None, scalars=(), after=()):
    arrays = [*scalars, *args, *after]
    specs = [in_smem] * len(scalars) + [in_vmem] * len(args) + [anywhere] * len(after)

    def run(*refs):
        given = len(scalars) + len(args)
        kernel(*refs[:given], *refs[given + len(after) :])

    return pl.pallas_call(
        run,
        in_specs=specs,
        out_specs=jax.tree.map(lambda _: in_vmem, out_shape),
        out_shape=out_shape,
        scratch_shapes=list(scratch),
        input_output_aliases=aliases or {},
        compiler_params=pltpu.CompilerParams(vmem_limit_bytes=14 * 2**20),
    )(*arrays)


def kept(x):
    return pltpu.with_memory_space_constraint(x, pltpu.VMEM)


def factor_of(values):
    return lax.rsqrt(jnp.mean(values * values, axis=-1, keepdims=True) + 1e-06)


def head_into(hidden_ref, gain, out_ref):
    for i in range(0, ROWS, STEP):
        values = hidden_ref[i : i + STEP, :].astype(f32)
        out_ref[i : i + STEP, :] = (values * factor_of(values) * gain).astype(bf16)


def scores_of(queries, docs):
    dims = (((1,), (1,)), ((), ()))
    return FACTOR * lax.dot_general(queries, docs, dims, preferred_element_type=f32)


def across(column):
    return jnp.broadcast_to(column, (ROWS, LANES))


def onehot_of(positives_ref):
    slots = lax.broadcasted_iota(jnp.int32, (ROWS, ROWS), 0)
    return (slots == positives_ref[...]).astype(f32).T


def gain_of(gain_ref):
    return jnp.concatenate([gain_ref[i : i + 1, :] for i in range(GAIN_ROWS)], axis=1)


def listed(neg_ref, distance):
    place, count = 0, 1
    for axis in AXES:
        place = place * lax.axis_size(axis) + lax.axis_index(axis)
        count = count * lax.axis_size(axis)
    sign = 1 - 2 * lax.rem(place, 2)
    block = lax.rem(place + sign * distance + count, count)
    found = neg_ref[0, 0] == block
    for i in range(1, neg_ref.shape[1]):
        found = jnp.logical_or(found, neg_ref[0, i] == block)
    return found


def own_kernel(q_ref, d_ref, gain_ref, pos_ref, qn_ref, dn_ref, s_ref, top_ref, total_ref, acc_ref, picked_ref):
    gain = gain_of(gain_ref)
    head_into(d_ref, gain, dn_ref)
    head_into(q_ref, gain, qn_ref)
    scores = scores_of(qn_ref[...], dn_ref[...])
    top = jnp.max(scores, axis=1, keepdims=True)
    probs = jnp.exp(scores - top)
    s_ref[...] = scores
    top_ref[...] = across(top)
    total_ref[...] = across(jnp.sum(probs, axis=1, keepdims=True))
    probs = probs.astype(bf16)
    onehot = onehot_of(pos_ref).astype(bf16)
    for c in range(0, WIDTH, CHUNK):
        docs = dn_ref[:, c : c + CHUNK]
        acc_ref[:, c : c + CHUNK] = jnp.dot(probs, docs, preferred_element_type=f32)
        picked_ref[:, c : c + CHUNK] = jnp.dot(onehot, docs, preferred_element_type=f32).astype(bf16)


def head_kernel(x_ref, gain_ref, out_ref):
    head_into(x_ref, gain_of(gain_ref), out_ref)


def fold(scores, dn_ref, top0_ref, total0_ref, acc0_ref):
    before = top0_ref[:, 0:1]
    top = jnp.maximum(before, jnp.max(scores, axis=1, keepdims=True))
    shrink = jnp.exp(before - top)
    probs = jnp.exp(scores - top)
    total = total0_ref[:, 0:1] * shrink + jnp.sum(probs, axis=1, keepdims=True)
    probs = probs.astype(bf16)

    def weighted(c):
        term = jnp.dot(probs, dn_ref[:, c : c + CHUNK], preferred_element_type=f32)
        return acc0_ref[:, c : c + CHUNK] * shrink + term

    return top, total, weighted


def step_kernel(distance, raw, neg_ref, x_ref, gain_ref, qn_ref, top0_ref, total0_ref, acc0_ref, s_ref, top_ref, total_ref, acc_ref, *scratch):
    dn_ref = x_ref
    if raw:
        dn_ref = scratch[0]
        head_into(x_ref, gain_of(gain_ref), dn_ref)
    scores = jnp.where(listed(neg_ref, distance), scores_of(qn_ref[...], dn_ref[...]), HIDDEN)
    top, total, weighted = fold(scores, dn_ref, top0_ref, total0_ref, acc0_ref)
    s_ref[...] = scores
    for c in range(0, WIDTH, CHUNK):
        acc_ref[:, c : c + CHUNK] = weighted(c)
    top_ref[...] = across(top)
    total_ref[...] = across(total)


def last_kernel(
    distance, neg_ref, dn_ref, q_ref, qn_ref, top0_ref, total0_ref, acc0_ref, picked_ref, pos_ref,
    s_own_ref, s_swap_ref, s_relay_ref, s_far_ref,
    gq_ref, part_ref, t_own_ref, t_near_ref, t_far_ref, t_back_ref, gain_sum,
):
    scores = jnp.where(listed(neg_ref, distance), scores_of(qn_ref[...], dn_ref[...]), HIDDEN)
    top, total, weighted = fold(scores, dn_ref, top0_ref, total0_ref, acc0_ref)
    lse = top + jnp.log(total)
    share = FACTOR / total
    onehot = onehot_of(pos_ref)
    loss = jnp.sum(lse - jnp.sum(s_own_ref[...] * onehot, axis=1, keepdims=True))

    for c in range(0, WIDTH, CHUNK):
        gq_ref[:, c : c + CHUNK] = weighted(c) * share - FACTOR * picked_ref[:, c : c + CHUNK].astype(f32)
    for i in range(0, ROWS, STEP):
        values = q_ref[i : i + STEP, :].astype(f32)
        added = gq_ref[i : i + STEP, :] * (values * factor_of(values))
        added = added[:8] + added[8:]
        gain_sum[...] = added if i == 0 else gain_sum[...] + added
    gain_part = 2.0 * jnp.sum(gain_sum[...], axis=0, keepdims=True)
    copies = part_ref.shape[0]
    for i in range(GAIN_ROWS):
        line = gain_part[:, i * LANES : (i + 1) * LANES]
        part_ref[:, i : i + 1, :] = jnp.broadcast_to(line[None], (copies, 1, LANES))
    part_ref[:, GAIN_ROWS:, :] = jnp.full((copies, SUM_ROWS - GAIN_ROWS, LANES), loss, f32)

    def turned(block_scores, less):
        weight = jnp.exp(block_scores - lse)
        weight = weight if less is None else weight - less
        return weight.T.astype(bf16)

    w_own = turned(s_own_ref[...], onehot)
    w_swap = turned(s_swap_ref[...], None)
    w_relay = turned(s_relay_ref[...], None)
    w_far = turned(s_far_ref[...], None)
    w_back = turned(scores, None)
    for c in range(0, WIDTH, CHUNK):
        cols = slice(c, c + CHUNK)
        queries = qn_ref[:, cols]

        def term(weight):
            return jnp.dot(weight, queries, preferred_element_type=f32)

        t_back_ref[:, cols] = term(w_back).astype(bf16)
        t_near_ref[0, :, cols] = term(w_relay).astype(bf16)
        t_near_ref[1, :, cols] = term(w_swap).astype(bf16)
        t_far_ref[:, cols] = term(w_far)
        t_own_ref[:, cols] = term(w_own)


def pull_into(values, gain, cotangent):
    factor = factor_of(values)
    scaled = gain * cotangent
    inner = jnp.sum(values * scaled, axis=-1, keepdims=True) / WIDTH
    return factor * scaled - values * (factor * factor * factor * inner)


def grad_query_kernel(q_ref, gain_ref, gq_ref, out_ref):
    gain = gain_of(gain_ref)
    for i in range(0, ROWS, STEP):
        rows = slice(i, i + STEP)
        out_ref[rows, :] = pull_into(q_ref[rows, :].astype(f32), gain, gq_ref[rows, :]).astype(bf16)


def grad_doc_kernel(d_ref, gain_ref, t_own_ref, near_ref, back_ref, far_ref, out_ref):
    gain = gain_of(gain_ref)
    for i in range(0, ROWS, STEP):
        rows = slice(i, i + STEP)
        total = t_own_ref[rows, :] + near_ref[1, rows, :].astype(f32)
        total = total + back_ref[rows, :].astype(f32) + far_ref[rows, :].astype(f32)
        out_ref[rows, :] = pull_into(d_ref[rows, :].astype(f32), gain, FACTOR * total).astype(bf16)


def add_kernel(t_far_ref, near_ref, out_ref):
    for i in range(0, ROWS, STEP):
        rows = slice(i, i + STEP)
        out_ref[rows, :] = (t_far_ref[rows, :] + near_ref[0, rows, :].astype(f32)).astype(bf16)


def sum_kernel(in_ref, out_ref):
    total = jnp.sum(in_ref[...], axis=0)
    out_ref[...] = jnp.broadcast_to(total[None], out_ref.shape)


def end_kernel(denom, in_ref, gain_ref, loss_ref):
    total = jnp.sum(in_ref[...], axis=0) / denom
    gain_ref[...] = total[:GAIN_ROWS]
    loss_ref[...] = total[GAIN_ROWS : GAIN_ROWS + 1, 0:1]


def body(query_hidden, doc_hidden, gain, positives, neg_blocks):
    count = lax.axis_size(AXES)
    gain = gain.reshape(GAIN_ROWS, LANES)
    positives = positives.reshape(1, ROWS)

    devices = range(count)
    far_source = [(i + 2 if i % 2 == 0 else i - 2) % count for i in devices]
    back_source = [(i - 2 if i % 2 == 0 else i + 2) % count for i in devices]

    def permute(x, route):
        return lax.ppermute(x, AXES, route)

    swap_route = [(i, i ^ 1) for i in devices]
    far = permute(doc_hidden, [(far_source[i], i) for i in devices])
    swap = permute(doc_hidden, swap_route)
    square, block = (ROWS, LANES), (ROWS, WIDTH)
    qn, dn, s_own, *state, picked = call(
        own_kernel,
        [held(block, bf16)] * 2 + [held(square, f32)] * 3 + [held(block, f32), held(block, bf16)],
        (query_hidden, doc_hidden, gain, positives),
    )
    qn, picked, s_own = kept(qn), kept(picked), kept(s_own)
    back = permute(dn, [(back_source[i], i) for i in devices])

    def step(distance, docs, state, raw=False):
        return call(
            functools.partial(step_kernel, distance, raw),
            [held(square, f32)] * 3 + [held(block, f32)],
            (docs, gain, qn, *map(kept, state)),
            scalars=(neg_blocks,),
            scratch=[pltpu.VMEM(block, bf16)] if raw else (),
            aliases={4: 1, 5: 2, 6: 3},
        )

    s_swap, *state = step(1, swap, state, raw=True)
    far = call(head_kernel, held(block, bf16), (far, gain), after=(s_swap,))
    relay = permute(far, swap_route)
    s_far, *state = step(2, far, state)
    s_relay, *state = step(-1, relay, state)
    sizes = [lax.axis_size(a) for a in AXES]
    gq, part, t_own, t_near, t_far, t_back = call(
        functools.partial(last_kernel, -2),
        [
            held(block, f32),
            held((sizes[0], SUM_ROWS, LANES), f32),
            held(block, f32),
            held((2, *block), bf16),
            held(block, f32),
            held(block, bf16),
        ],
        (back, query_hidden, qn, *map(kept, state), picked, positives, s_own, kept(s_swap), kept(s_relay), kept(s_far)),
        scalars=(neg_blocks,),
        scratch=[pltpu.VMEM((8, WIDTH), f32)],
        aliases={6: 0},
    )
    back_term = permute(t_back, [(i, back_source[i]) for i in devices])
    near_term = permute(t_near, swap_route)

    part = lax.all_to_all(part, AXES[0], 0, 0, tiled=True)
    part = call(sum_kernel, held((sizes[1], SUM_ROWS, LANES), f32), (part,))
    far_sum = call(add_kernel, held(block, bf16), (kept(t_far), near_term), after=(part,))
    far_term = permute(far_sum, [(i, far_source[i]) for i in devices])
    part = lax.all_to_all(part, AXES[1], 0, 0, tiled=True)
    part = call(sum_kernel, held((sizes[2], SUM_ROWS, LANES), f32), (part,))
    part = lax.all_to_all(part, AXES[2], 0, 0, tiled=True)
    grad = jax.ShapeDtypeStruct(block, bf16)
    grad_query = call(grad_query_kernel, grad, (query_hidden, gain, kept(gq)))
    grad_doc = call(grad_doc_kernel, grad, (doc_hidden, gain, kept(t_own), near_term, back_term, far_term))
    grad_gain, mean_loss = call(
        functools.partial(end_kernel, float(ROWS * count)),
        [jax.ShapeDtypeStruct((GAIN_ROWS, LANES), f32), jax.ShapeDtypeStruct((1, 1), f32)],
        (part,),
    )
    return mean_loss.reshape(()), grad_gain.reshape(WIDTH), grad_query, grad_doc


def grid_of(count):
    return (8, 12, 8) if count == 768 else (2, count // 16, 8)


def solution(mesh):
    devices = np.asarray(mesh.devices)
    inner = Mesh(devices.reshape(grid_of(devices.size)), AXES)
    placed = (P(AXES, None), P(AXES, None), P(), P(AXES), P(AXES, None))
    return jax.shard_map(
        body,
        mesh=inner,
        in_specs=placed,
        out_specs=(P(), P(), P(AXES, None), P(AXES, None)),
        check_vma=False,
    )
```

```python
import functools
import math

import jax
import jax.numpy as jnp
import numpy as np
from jax import lax
from jax.experimental import pallas as pl
from jax.experimental.pallas import tpu as pltpu
from jax.sharding import Mesh
from jax.sharding import PartitionSpec as P

logit_scale = 4.0
ROWS = 128
WIDTH = 3584
FACTOR = logit_scale / math.sqrt(WIDTH)
LANES = 128
GAIN_ROWS = WIDTH // LANES
SUM_ROWS = 32
CHUNK = 512
HIDDEN = -1e30
STEP = 16
PARTS = 4
PART = ROWS // PARTS
f32, bf16 = jnp.float32, jnp.bfloat16
AXES = ("y", "z", "row")

in_vmem = pl.BlockSpec(memory_space=pltpu.VMEM)
anywhere = pl.BlockSpec(memory_space=pl.ANY)
in_smem = pl.BlockSpec(memory_space=pltpu.SMEM)


def held(shape, dtype):
    return pltpu.VMEM(shape, dtype)


def call(kernel, out_shape, args, scratch=(), aliases=None, scalars=(), distant=(), after=()):
    given = len(scalars) + len(args) + len(distant)

    def run(*refs):
        kernel(*refs[:given], *refs[given + len(after) :])

    flat, tree = jax.tree.flatten(out_shape)
    outs = [anywhere if is_distant(x) else in_vmem for x in flat]
    return pl.pallas_call(
        run,
        in_specs=[in_smem] * len(scalars) + [in_vmem] * len(args) + [anywhere] * (len(distant) + len(after)),
        out_specs=jax.tree.unflatten(tree, outs),
        out_shape=out_shape,
        scratch_shapes=list(scratch),
        input_output_aliases=aliases or {},
        cost_estimate=pl.CostEstimate(flops=1000, bytes_accessed=1000, transcendentals=0),
        compiler_params=pltpu.CompilerParams(vmem_limit_bytes=15 * 2**20),
    )(*scalars, *args, *distant, *after)


def kept(x):
    return pltpu.with_memory_space_constraint(x, pltpu.VMEM)


def leave(x):
    return pltpu.with_memory_space_constraint(x, pltpu.HBM)


def distant_array(shape, dtype):
    return pltpu.HBM(shape, dtype)


def is_distant(shape):
    return getattr(shape, "memory_space", None) == pltpu.HBM


def factor_of(values):
    return lax.rsqrt(jnp.mean(values * values, axis=-1, keepdims=True) + 1e-06)


def head_into(hidden_ref, gain, out_ref):
    for i in range(0, ROWS, STEP):
        values = hidden_ref[i : i + STEP, :].astype(f32)
        out_ref[i : i + STEP, :] = (values * factor_of(values) * gain).astype(bf16)


def scores_of(queries, docs):
    dims = (((1,), (1,)), ((), ()))
    return FACTOR * lax.dot_general(queries, docs, dims, preferred_element_type=f32)


def across(column):
    return jnp.broadcast_to(column, (ROWS, LANES))


def onehot_of(positives_ref):
    slots = lax.broadcasted_iota(jnp.int32, (ROWS, ROWS), 0)
    return (slots == positives_ref[...]).astype(f32).T


def listed(neg_ref, distance):
    place, count = 0, 1
    for axis in AXES:
        place = place * lax.axis_size(axis) + lax.axis_index(axis)
        count = count * lax.axis_size(axis)
    sign = 1 - 2 * lax.rem(place, 2)
    block = lax.rem(place + sign * distance + count, count)
    found = neg_ref[0, 0] == block
    for i in range(1, neg_ref.shape[1]):
        found = jnp.logical_or(found, neg_ref[0, i] == block)
    return found


def own_kernel(
    q_hbm, d_hbm, gain_hbm, pos_hbm,
    qn_ref, dn_ref, gain_ref, s_ref, top_ref, total_ref, acc_ref, picked_ref,
    q_ref, d_ref, line_ref, pos_ref, sems,
):
    pairs = ((d_hbm, d_ref), (gain_hbm, line_ref), (q_hbm, q_ref), (pos_hbm, pos_ref))
    copies = [pltpu.make_async_copy(src, dst, sems.at[i]) for i, (src, dst) in enumerate(pairs)]
    for copy in copies:
        copy.start()
    copies[0].wait()
    copies[1].wait()
    gain = jnp.concatenate([line_ref[i : i + 1, :] for i in range(GAIN_ROWS)], axis=1)
    gain_ref[...] = gain
    head_into(d_ref, gain, dn_ref)
    copies[2].wait()
    copies[3].wait()
    head_into(q_ref, gain, qn_ref)
    scores = scores_of(qn_ref[...], dn_ref[...])
    top = jnp.max(scores, axis=1, keepdims=True)
    probs = jnp.exp(scores - top)
    s_ref[...] = scores
    top_ref[...] = across(top)
    total_ref[...] = across(jnp.sum(probs, axis=1, keepdims=True))
    probs = probs.astype(bf16)
    onehot = onehot_of(pos_ref).astype(bf16)
    for c in range(0, WIDTH, CHUNK):
        docs = dn_ref[:, c : c + CHUNK]
        acc_ref[:, c : c + CHUNK] = jnp.dot(probs, docs, preferred_element_type=f32)
        picked_ref[:, c : c + CHUNK] = jnp.dot(onehot, docs, preferred_element_type=f32).astype(bf16)


def head_kernel(x_ref, gain_ref, out_ref):
    head_into(x_ref, gain_ref[...], out_ref)


def fold(scores, dn_ref, top0_ref, total0_ref, acc0_ref):
    before = top0_ref[:, 0:1]
    top = jnp.maximum(before, jnp.max(scores, axis=1, keepdims=True))
    shrink = jnp.exp(before - top)
    probs = jnp.exp(scores - top)
    total = total0_ref[:, 0:1] * shrink + jnp.sum(probs, axis=1, keepdims=True)
    probs = probs.astype(bf16)

    def weighted(c):
        term = jnp.dot(probs, dn_ref[:, c : c + CHUNK], preferred_element_type=f32)
        return acc0_ref[:, c : c + CHUNK] * shrink + term

    return top, total, weighted


def step_kernel(distance, neg_ref, dn_ref, qn_ref, top0_ref, total0_ref, acc0_ref, s_ref, top_ref, total_ref, acc_ref):
    scores = jnp.where(listed(neg_ref, distance), scores_of(qn_ref[...], dn_ref[...]), HIDDEN)
    top, total, weighted = fold(scores, dn_ref, top0_ref, total0_ref, acc0_ref)
    s_ref[...] = scores
    for c in range(0, WIDTH, CHUNK):
        acc_ref[:, c : c + CHUNK] = weighted(c)
    top_ref[...] = across(top)
    total_ref[...] = across(total)


def last_kernel(
    distance, neg_ref, dn_ref, qn_ref, top0_ref, total0_ref, acc0_ref, picked_ref, s_own_ref, pos_hbm, q_hbm,
    s_ref, lse_ref, gq_ref, hot_ref, part_ref, q_ref, pos_ref, gain_sum, sems,
):
    copies = [pltpu.make_async_copy(q_hbm, q_ref, sems.at[0]), pltpu.make_async_copy(pos_hbm, pos_ref, sems.at[1])]
    for copy in copies:
        copy.start()
    scores = jnp.where(listed(neg_ref, distance), scores_of(qn_ref[...], dn_ref[...]), HIDDEN)
    top, total, weighted = fold(scores, dn_ref, top0_ref, total0_ref, acc0_ref)
    lse = top + jnp.log(total)
    s_ref[...] = scores
    lse_ref[...] = across(lse)
    for copy in copies:
        copy.wait()
    onehot = onehot_of(pos_ref)
    hot_ref[...] = onehot
    loss = jnp.sum(lse - jnp.sum(s_own_ref[...] * onehot, axis=1, keepdims=True))
    share = FACTOR / total
    for c in range(0, WIDTH, CHUNK):
        gq_ref[:, c : c + CHUNK] = weighted(c) * share - FACTOR * picked_ref[:, c : c + CHUNK].astype(f32)
    for i in range(0, ROWS, STEP):
        values = q_ref[i : i + STEP, :].astype(f32)
        added = gq_ref[i : i + STEP, :] * (values * factor_of(values))
        added = added[:8] + added[8:]
        gain_sum[...] = added if i == 0 else gain_sum[...] + added
    gain_part = 2.0 * jnp.sum(gain_sum[...], axis=0, keepdims=True)
    share_rows = part_ref.shape[1]
    for i in range(GAIN_ROWS):
        line = gain_part[:, i * LANES : (i + 1) * LANES]
        part_ref[i // share_rows, i % share_rows : i % share_rows + 1, :] = line
    for i in range(GAIN_ROWS, SUM_ROWS):
        part_ref[i // share_rows, i % share_rows : i % share_rows + 1, :] = jnp.full((1, LANES), loss, f32)


def term_kernel(
    qn_ref, gain_ref, gq_ref, lse_ref, hot_ref, s_own_ref, s_swap_ref, s_relay_ref, s_far_ref, s_back_ref, q_hbm,
    near_hbm, back_hbm, far_hbm, own_hbm, grad_hbm, q_ref, grad_ref, weight_ref, term_ref, sems, row_sems,
):
    incoming = pltpu.make_async_copy(q_hbm, q_ref, sems.at[0])
    incoming.start()
    blocks = (s_relay_ref, s_swap_ref, s_back_ref, s_far_ref, s_own_ref)
    for k, block_ref in enumerate(blocks):
        weight = jnp.exp(block_ref[...] - lse_ref[...])
        if block_ref is s_own_ref:
            weight = weight - hot_ref[...]
        weight_ref[k * ROWS : (k + 1) * ROWS, :] = weight.T.astype(bf16)
    targets = (near_hbm.at[0], near_hbm.at[1], back_hbm, far_hbm, own_hbm)
    outgoing = []
    for k, target in enumerate(targets):
        weight = weight_ref[k * ROWS : (k + 1) * ROWS, :]
        for c in range(0, WIDTH, CHUNK):
            cols = slice(c, c + CHUNK)
            term_ref[k, :, cols] = jnp.dot(weight, qn_ref[:, cols], preferred_element_type=f32).astype(bf16)
        copy = pltpu.make_async_copy(term_ref.at[k], target, sems.at[k + 1])
        copy.start()
        outgoing.append(copy)
    incoming.wait()
    gain = gain_ref[...]
    for part in range(PARTS):
        for i in range(part * PART, (part + 1) * PART, STEP):
            rows = slice(i, i + STEP)
            grad_ref[rows, :] = pull(q_ref[rows, :].astype(f32), gain, gq_ref[rows, :]).astype(bf16)
        rows = pl.ds(part * PART, PART)
        copy = pltpu.make_async_copy(grad_ref.at[rows, :], grad_hbm.at[rows, :], row_sems.at[part])
        copy.start()
        outgoing.append(copy)
    for copy in outgoing:
        copy.wait()


def pull(values, gain, cotangent):
    factor = factor_of(values)
    scaled = gain * cotangent
    inner = jnp.sum(values * scaled, axis=-1, keepdims=True) / WIDTH
    return factor * scaled - values * (factor * factor * factor * inner)


def by_parts(sources, target, buffers, out_ref, sems, work):
    def copies(part):
        rows = pl.ds(part * PART, PART)
        return [
            pltpu.make_async_copy(source.at[rows, :], buffers.at[k, rows, :], sems.at[k, part])
            for k, source in enumerate(sources)
        ]

    incoming = [copies(part) for part in range(PARTS)]
    for part in incoming:
        for copy in part:
            copy.start()
    outgoing = []
    for part in range(PARTS):
        for copy in incoming[part]:
            copy.wait()
        for i in range(part * PART, (part + 1) * PART, STEP):
            rows = slice(i, i + STEP)
            out_ref[rows, :] = work(*[buffers[k, rows, :].astype(f32) for k in range(len(sources))]).astype(bf16)
        rows = pl.ds(part * PART, PART)
        copy = pltpu.make_async_copy(out_ref.at[rows, :], target.at[rows, :], sems.at[len(sources), part])
        copy.start()
        outgoing.append(copy)
    for copy in outgoing:
        copy.wait()


def grad_doc_kernel(gain_ref, d_hbm, own_hbm, near_hbm, back_hbm, far_hbm, grad_hbm, buffers, out_ref, sems):
    gain = gain_ref[...]

    def work(values, own, near, back, far):
        return pull(values, gain, FACTOR * (own + near + back + far))

    by_parts((d_hbm, own_hbm, near_hbm.at[1], back_hbm, far_hbm), grad_hbm, buffers, out_ref, sems, work)


def add_kernel(far_hbm, near_hbm, sum_hbm, buffers, out_ref, sems):
    by_parts((far_hbm, near_hbm.at[0]), sum_hbm, buffers, out_ref, sems, lambda far, near: far + near)


def sum_kernel(in_ref, out_ref):
    total = jnp.sum(in_ref[...], axis=0)
    out_ref[...] = jnp.broadcast_to(total[None], out_ref.shape)


def end_kernel(denom, in_ref, gain_ref, loss_ref):
    rows = in_ref.shape[1]
    total = in_ref[...] / denom
    for i in range(GAIN_ROWS):
        gain_ref[i : i + 1, :] = total[i // rows, i % rows : i % rows + 1, :]
    loss_ref[...] = total[GAIN_ROWS // rows, GAIN_ROWS % rows : GAIN_ROWS % rows + 1, 0:1]


def body(query_hidden, doc_hidden, gain, positives, neg_blocks):
    count = lax.axis_size(AXES)
    gain = gain.reshape(GAIN_ROWS, LANES)
    positives = positives.reshape(1, ROWS)

    devices = range(count)
    far_source = [(i + 2 if i % 2 == 0 else i - 2) % count for i in devices]
    back_source = [(i - 2 if i % 2 == 0 else i + 2) % count for i in devices]

    def permute(x, route):
        return lax.ppermute(x, AXES, route)

    swap_route = [(i, i ^ 1) for i in devices]
    square, block = (ROWS, LANES), (ROWS, WIDTH)
    dma = pltpu.SemaphoreType.DMA
    far = permute(doc_hidden, [(far_source[i], i) for i in devices])
    qn, dn, gain_line, s_own, *state, picked = call(
        own_kernel,
        [held(block, bf16)] * 2
        + [held((1, WIDTH), f32)]
        + [held(square, f32)] * 3
        + [held(block, f32), held(block, bf16)],
        (),
        distant=(leave(query_hidden), leave(doc_hidden), leave(gain), leave(positives)),
        scratch=[
            pltpu.VMEM(block, bf16), pltpu.VMEM(block, bf16), pltpu.VMEM((GAIN_ROWS, LANES), f32),
            pltpu.VMEM((1, ROWS), jnp.int32), dma((4,)),
        ],
    )
    qn, gain_line, picked, s_own = kept(qn), kept(gain_line), kept(picked), kept(s_own)
    back = permute(dn, [(back_source[i], i) for i in devices])
    swap = permute(dn, swap_route)

    def step(distance, docs, state):
        return call(
            functools.partial(step_kernel, distance),
            [held(square, f32)] * 3 + [held(block, f32)],
            (docs, qn, *map(kept, state)),
            scalars=(neg_blocks,),
            aliases={3: 1, 4: 2, 5: 3},
        )

    far = call(head_kernel, held(block, bf16), (far, gain_line))
    relay = permute(far, swap_route)
    s_swap, *state = step(1, swap, state)
    s_far, *state = step(2, far, state)
    s_back, *state = step(-2, back, state)
    sizes = [lax.axis_size(a) for a in AXES]
    share = (SUM_ROWS // sizes[2], LANES)
    s_relay, lse, gq, hot, part = call(
        functools.partial(last_kernel, -1),
        [held(square, f32)] * 2 + [held(block, f32), held(square, f32), held((sizes[2], *share), f32)],
        (relay, qn, *map(kept, state), picked, s_own),
        scalars=(neg_blocks,),
        distant=(leave(positives), leave(query_hidden)),
        scratch=[pltpu.VMEM(block, bf16), pltpu.VMEM((1, ROWS), jnp.int32), pltpu.VMEM((8, WIDTH), f32), dma((2,))],
        aliases={5: 2},
    )

    def exchange(x, axis):
        return kept(lax.all_to_all(x, AXES[axis], 0, 0, tiled=True))

    def summed(x, axis):
        return call(sum_kernel, held((sizes[axis], *share), f32), (x,))

    part = summed(exchange(part, 2), 0)
    t_near, t_back, t_far, t_own, grad_query = call(
        term_kernel,
        [distant_array((2, *block), bf16)] + [distant_array(block, bf16)] * 4,
        (qn, gain_line, kept(gq), kept(lse), kept(hot), s_own, kept(s_swap), kept(s_relay), kept(s_far), kept(s_back)),
        distant=(leave(query_hidden),),
        after=(part,),
        scratch=[
            pltpu.VMEM(block, bf16), pltpu.VMEM(block, bf16), pltpu.VMEM((5 * ROWS, ROWS), bf16),
            pltpu.VMEM((5, *block), bf16), dma((6,)), dma((PARTS,)),
        ],
    )
    near_term = permute(t_near, swap_route)
    back_term = permute(t_back, [(i, back_source[i]) for i in devices])

    part = summed(exchange(part, 0), 1)
    far_sum = call(
        add_kernel,
        distant_array(block, bf16),
        (),
        distant=(leave(t_far), near_term),
        after=(part,),
        scratch=[pltpu.VMEM((2, *block), bf16), pltpu.VMEM(block, bf16), dma((3, PARTS))],
    )
    far_term = permute(far_sum, [(i, far_source[i]) for i in devices])
    part = summed(exchange(part, 1), 2)
    part = exchange(part, 2)
    grad_doc = call(
        grad_doc_kernel,
        distant_array(block, bf16),
        (gain_line,),
        distant=(leave(doc_hidden), leave(t_own), near_term, back_term, far_term),
        scratch=[pltpu.VMEM((5, *block), bf16), pltpu.VMEM(block, bf16), dma((6, PARTS))],
    )
    grad_gain, mean_loss = call(
        functools.partial(end_kernel, float(ROWS * count)),
        [jax.ShapeDtypeStruct((GAIN_ROWS, LANES), f32), jax.ShapeDtypeStruct((1, 1), f32)],
        (part,),
    )
    return mean_loss.reshape(()), grad_gain.reshape(WIDTH), grad_query, grad_doc


def grid_of(count):
    return (8, 12, 8) if count == 768 else (2, count // 16, 8)


def solution(mesh):
    devices = np.asarray(mesh.devices)
    inner = Mesh(devices.reshape(grid_of(devices.size)), AXES)
    placed = (P(AXES, None), P(AXES, None), P(), P(AXES), P(AXES, None))
    return jax.shard_map(
        body,
        mesh=inner,
        in_specs=placed,
        out_specs=(P(), P(), P(AXES, None), P(AXES, None)),
        check_vma=False,
    )
```

```python
import functools
import math

import jax
import jax.numpy as jnp
import numpy as np
from jax import lax
from jax.experimental import pallas as pl
from jax.experimental.pallas import tpu as pltpu
from jax.sharding import Mesh
from jax.sharding import PartitionSpec as P

logit_scale = 4.0
ROWS = 128
WIDTH = 3584
FACTOR = logit_scale / math.sqrt(WIDTH)
LANES = 128
GAIN_ROWS = WIDTH // LANES
SUM_ROWS = 32
CHUNK = 512
HIDDEN = -1e30
STEP = 16
PARTS = 4
TERM_FLOPS, ADD_FLOPS, GRAD_FLOPS = 3_000_000_000, 1_500_000_000, 3_000_000_000
PART = ROWS // PARTS
f32, bf16 = jnp.float32, jnp.bfloat16
AXES = ("y", "z", "row")

in_vmem = pl.BlockSpec(memory_space=pltpu.VMEM)
anywhere = pl.BlockSpec(memory_space=pl.ANY)
in_smem = pl.BlockSpec(memory_space=pltpu.SMEM)


def held(shape, dtype):
    return pltpu.VMEM(shape, dtype)


def call(kernel, out_shape, args, scratch=(), aliases=None, scalars=(), distant=(), after=(), flops=1000):
    given = len(scalars) + len(args) + len(distant)

    def run(*refs):
        kernel(*refs[:given], *refs[given + len(after) :])

    flat, tree = jax.tree.flatten(out_shape)
    outs = [anywhere if is_distant(x) else in_vmem for x in flat]
    return pl.pallas_call(
        run,
        in_specs=[in_smem] * len(scalars) + [in_vmem] * len(args) + [anywhere] * (len(distant) + len(after)),
        out_specs=jax.tree.unflatten(tree, outs),
        out_shape=out_shape,
        scratch_shapes=list(scratch),
        input_output_aliases=aliases or {},
        cost_estimate=pl.CostEstimate(flops=flops, bytes_accessed=1000, transcendentals=0),
        compiler_params=pltpu.CompilerParams(vmem_limit_bytes=15 * 2**20),
    )(*scalars, *args, *distant, *after)


def kept(x):
    return pltpu.with_memory_space_constraint(x, pltpu.VMEM)


def leave(x):
    return pltpu.with_memory_space_constraint(x, pltpu.HBM)


def distant_array(shape, dtype):
    return pltpu.HBM(shape, dtype)


def is_distant(shape):
    return getattr(shape, "memory_space", None) == pltpu.HBM


def factor_of(values):
    return lax.rsqrt(jnp.mean(values * values, axis=-1, keepdims=True) + 1e-06)


def head_into(hidden_ref, gain, out_ref):
    for i in range(0, ROWS, STEP):
        values = hidden_ref[i : i + STEP, :].astype(f32)
        out_ref[i : i + STEP, :] = (values * factor_of(values) * gain).astype(bf16)


def scores_of(queries, docs):
    dims = (((1,), (1,)), ((), ()))
    return FACTOR * lax.dot_general(queries, docs, dims, preferred_element_type=f32)


def across(column):
    return jnp.broadcast_to(column, (ROWS, LANES))


def onehot_of(positives_ref):
    slots = lax.broadcasted_iota(jnp.int32, (ROWS, ROWS), 0)
    return (slots == positives_ref[...]).astype(f32).T


def listed(neg_ref, distance):
    place, count = 0, 1
    for axis in AXES:
        place = place * lax.axis_size(axis) + lax.axis_index(axis)
        count = count * lax.axis_size(axis)
    sign = 1 - 2 * lax.rem(place, 2)
    block = lax.rem(place + sign * distance + count, count)
    found = neg_ref[0, 0] == block
    for i in range(1, neg_ref.shape[1]):
        found = jnp.logical_or(found, neg_ref[0, i] == block)
    return found


def own_kernel(
    q_hbm, d_hbm, gain_hbm, pos_hbm,
    qn_ref, dn_ref, gain_ref, s_ref, top_ref, total_ref, acc_ref, picked_ref,
    q_ref, d_ref, line_ref, pos_ref, sems,
):
    pairs = ((d_hbm, d_ref), (gain_hbm, line_ref), (q_hbm, q_ref), (pos_hbm, pos_ref))
    copies = [pltpu.make_async_copy(src, dst, sems.at[i]) for i, (src, dst) in enumerate(pairs)]
    for copy in copies:
        copy.start()
    copies[0].wait()
    copies[1].wait()
    gain = jnp.concatenate([line_ref[i : i + 1, :] for i in range(GAIN_ROWS)], axis=1)
    gain_ref[...] = gain
    head_into(d_ref, gain, dn_ref)
    copies[2].wait()
    copies[3].wait()
    head_into(q_ref, gain, qn_ref)
    scores = scores_of(qn_ref[...], dn_ref[...])
    top = jnp.max(scores, axis=1, keepdims=True)
    probs = jnp.exp(scores - top)
    s_ref[...] = scores
    top_ref[...] = across(top)
    total_ref[...] = across(jnp.sum(probs, axis=1, keepdims=True))
    probs = probs.astype(bf16)
    onehot = onehot_of(pos_ref).astype(bf16)
    for c in range(0, WIDTH, CHUNK):
        docs = dn_ref[:, c : c + CHUNK]
        acc_ref[:, c : c + CHUNK] = jnp.dot(probs, docs, preferred_element_type=f32)
        picked_ref[:, c : c + CHUNK] = jnp.dot(onehot, docs, preferred_element_type=f32).astype(bf16)


def head_kernel(x_ref, gain_ref, out_ref):
    head_into(x_ref, gain_ref[...], out_ref)


def fold(blocks, top0_ref, total0_ref):
    before = top0_ref[:, 0:1]
    top = before
    for scores in blocks:
        top = jnp.maximum(top, jnp.max(scores, axis=1, keepdims=True))
    shrink = jnp.exp(before - top)
    total = total0_ref[:, 0:1] * shrink
    probs = []
    for scores in blocks:
        prob = jnp.exp(scores - top)
        total = total + jnp.sum(prob, axis=1, keepdims=True)
        probs.append(prob.astype(bf16))
    return top, total, shrink, probs


def pair_kernel(
    distances, neg_ref, swap_ref, far_ref, qn_ref, top0_ref, total0_ref, acc0_ref,
    s_swap_ref, s_far_ref, top_ref, total_ref, acc_ref,
):
    for distance, dn_ref, s_ref in zip(distances, (swap_ref, far_ref), (s_swap_ref, s_far_ref)):
        s_ref[...] = jnp.where(listed(neg_ref, distance), scores_of(qn_ref[...], dn_ref[...]), HIDDEN)
    top, total, shrink, probs = fold((s_swap_ref[...], s_far_ref[...]), top0_ref, total0_ref)
    for c in range(0, WIDTH, CHUNK):
        cols = slice(c, c + CHUNK)
        term = jnp.dot(probs[0], swap_ref[:, cols], preferred_element_type=f32)
        term = term + jnp.dot(probs[1], far_ref[:, cols], preferred_element_type=f32)
        acc_ref[:, cols] = acc0_ref[:, cols] * shrink + term
    top_ref[...] = across(top)
    total_ref[...] = across(total)


def score_kernel(distance, neg_ref, dn_ref, qn_ref, s_ref):
    s_ref[...] = jnp.where(listed(neg_ref, distance), scores_of(qn_ref[...], dn_ref[...]), HIDDEN)


def last_kernel(
    distance, neg_ref, dn_ref, back_ref, s_back_ref, qn_ref, top0_ref, total0_ref, acc0_ref, picked_ref, s_own_ref,
    pos_hbm, q_hbm,
    s_ref, lse_ref, gq_ref, hot_ref, part_ref, q_ref, pos_ref, lines, sems,
):
    copies = [pltpu.make_async_copy(q_hbm, q_ref, sems.at[0]), pltpu.make_async_copy(pos_hbm, pos_ref, sems.at[1])]
    for copy in copies:
        copy.start()
    scores = jnp.where(listed(neg_ref, distance), scores_of(qn_ref[...], dn_ref[...]), HIDDEN)
    top, total, shrink, (probs, back_probs) = fold((scores, s_back_ref[...]), top0_ref, total0_ref)
    lse = top + jnp.log(total)
    s_ref[...] = scores
    lse_ref[...] = across(lse)
    for copy in copies:
        copy.wait()
    onehot = onehot_of(pos_ref)
    hot_ref[...] = onehot
    loss = jnp.sum(lse - jnp.sum(s_own_ref[...] * onehot, axis=1, keepdims=True))
    share = FACTOR / total
    kept_share = shrink * share
    squares = [
        jnp.sum(jnp.square(q_ref[i : i + STEP, :].astype(f32)), axis=-1, keepdims=True) for i in range(0, ROWS, STEP)
    ]
    factor = lax.rsqrt(jnp.concatenate(squares, axis=0) / WIDTH + 1e-06)
    for c in range(0, WIDTH, CHUNK):
        cols = slice(c, c + CHUNK)
        term = jnp.dot(probs, dn_ref[:, cols], preferred_element_type=f32)
        term = term + jnp.dot(back_probs, back_ref[:, cols], preferred_element_type=f32)
        gq = acc0_ref[:, cols] * kept_share + term * share - FACTOR * picked_ref[:, cols].astype(f32)
        gq_ref[:, cols] = gq
        added = 2.0 * jnp.sum(gq * (q_ref[:, cols].astype(f32) * factor), axis=0, keepdims=True)
        for i in range(0, CHUNK, LANES):
            lines[(c + i) // LANES : (c + i) // LANES + 1, :] = added[:, i : i + LANES]
    lines[GAIN_ROWS:, :] = jnp.full((SUM_ROWS - GAIN_ROWS, LANES), loss, f32)
    part_ref[...] = jnp.broadcast_to(lines[...][None], part_ref.shape)


def term_kernel(
    qn_ref, gain_ref, gq_ref, lse_ref, hot_ref, s_own_ref, s_swap_ref, s_relay_ref, s_far_ref, s_back_ref, q_hbm,
    near_hbm, back_hbm, far_hbm, own_hbm, grad_hbm, q_ref, grad_ref, weight_ref, term_ref, scaled_ref, sems, row_sems,
):
    incoming = pltpu.make_async_copy(q_hbm, q_ref, sems.at[0])
    incoming.start()
    blocks = (s_relay_ref, s_swap_ref, s_back_ref, s_far_ref, s_own_ref)
    for k, block_ref in enumerate(blocks):
        weight = jnp.exp(block_ref[...] - lse_ref[...])
        if block_ref is s_own_ref:
            weight = weight - hot_ref[...]
        weight_ref[k * ROWS : (k + 1) * ROWS, :] = weight.T.astype(bf16)
    targets = (near_hbm.at[0], near_hbm.at[1], back_hbm, far_hbm, own_hbm)
    outgoing = []
    for k, target in enumerate(targets):
        weight = weight_ref[k * ROWS : (k + 1) * ROWS, :]
        for c in range(0, WIDTH, CHUNK):
            cols = slice(c, c + CHUNK)
            term_ref[k, :, cols] = jnp.dot(weight, qn_ref[:, cols], preferred_element_type=f32).astype(bf16)
        copy = pltpu.make_async_copy(term_ref.at[k], target, sems.at[k + 1])
        copy.start()
        outgoing.append(copy)
    incoming.wait()

    def values_at(rows, cols):
        return q_ref[rows, cols].astype(f32)

    def cotangent_at(rows, cols):
        return gq_ref[rows, cols]

    for part in range(PARTS):
        for i in range(part * PART, (part + 1) * PART, STEP):
            pull(values_at, cotangent_at, gain_ref, scaled_ref, grad_ref, slice(i, i + STEP))
        rows = pl.ds(part * PART, PART)
        copy = pltpu.make_async_copy(grad_ref.at[rows, :], grad_hbm.at[rows, :], row_sems.at[part])
        copy.start()
        outgoing.append(copy)
    for copy in outgoing:
        copy.wait()


def pull(values_at, cotangent_at, gain_ref, scaled_ref, out_ref, rows):
    square = jnp.zeros((STEP, CHUNK), f32)
    inner = jnp.zeros((STEP, CHUNK), f32)
    chunks = [slice(c, c + CHUNK) for c in range(0, WIDTH, CHUNK)]
    for cols in chunks:
        values = values_at(rows, cols)
        scaled = gain_ref[:, cols] * cotangent_at(rows, cols)
        scaled_ref[:, cols] = scaled
        square = square + values * values
        inner = inner + values * scaled
    factor = lax.rsqrt(jnp.sum(square, axis=-1, keepdims=True) / WIDTH + 1e-06)
    inner = factor * factor * factor * (jnp.sum(inner, axis=-1, keepdims=True) / WIDTH)
    for cols in chunks:
        grad = factor * scaled_ref[:, cols] - values_at(rows, cols) * inner
        out_ref[rows, cols] = grad.astype(bf16)


def by_parts(sources, target, buffers, out_ref, sems, work):
    def copies(part):
        rows = pl.ds(part * PART, PART)
        return [
            pltpu.make_async_copy(source.at[rows, :], buffers.at[k, rows, :], sems.at[k, part])
            for k, source in enumerate(sources)
        ]

    incoming = [copies(part) for part in range(PARTS)]
    for part in incoming:
        for copy in part:
            copy.start()
    outgoing = []
    for part in range(PARTS):
        for copy in incoming[part]:
            copy.wait()
        for i in range(part * PART, (part + 1) * PART, STEP):
            work(slice(i, i + STEP))
        rows = pl.ds(part * PART, PART)
        copy = pltpu.make_async_copy(out_ref.at[rows, :], target.at[rows, :], sems.at[len(sources), part])
        copy.start()
        outgoing.append(copy)
    for copy in outgoing:
        copy.wait()


def grad_doc_kernel(gain_ref, d_hbm, own_hbm, near_hbm, back_hbm, far_hbm, grad_hbm, buffers, out_ref, scaled_ref, sems):
    def at(k, rows, cols):
        return buffers[k, rows, cols].astype(f32)

    def cotangent_at(rows, cols):
        return FACTOR * ((at(1, rows, cols) + at(2, rows, cols)) + (at(3, rows, cols) + at(4, rows, cols)))

    def work(rows):
        pull(functools.partial(at, 0), cotangent_at, gain_ref, scaled_ref, out_ref, rows)

    by_parts((d_hbm, own_hbm, near_hbm.at[1], back_hbm, far_hbm), grad_hbm, buffers, out_ref, sems, work)


def add_kernel(far_hbm, near_hbm, sum_hbm, buffers, out_ref, sems):
    def work(rows):
        for c in range(0, WIDTH, CHUNK):
            cols = slice(c, c + CHUNK)
            total = buffers[0, rows, cols].astype(f32) + buffers[1, rows, cols].astype(f32)
            out_ref[rows, cols] = total.astype(bf16)

    by_parts((far_hbm, near_hbm.at[0]), sum_hbm, buffers, out_ref, sems, work)


def sum_kernel(in_ref, out_ref):
    total = jnp.sum(in_ref[...], axis=0)
    out_ref[...] = jnp.broadcast_to(total[None], out_ref.shape)


def end_kernel(denom, in_ref, gain_ref, loss_ref):
    total = jnp.sum(in_ref[...], axis=0) / denom
    gain_ref[...] = total[:GAIN_ROWS]
    loss_ref[...] = total[GAIN_ROWS : GAIN_ROWS + 1, 0:1]


def body(query_hidden, doc_hidden, gain, positives, neg_blocks):
    count = lax.axis_size(AXES)
    gain = gain.reshape(GAIN_ROWS, LANES)
    positives = positives.reshape(1, ROWS)

    devices = range(count)
    far_source = [(i + 2 if i % 2 == 0 else i - 2) % count for i in devices]
    back_source = [(i - 2 if i % 2 == 0 else i + 2) % count for i in devices]

    def permute(x, route):
        return lax.ppermute(x, AXES, route)

    swap_route = [(i, i ^ 1) for i in devices]
    square, block = (ROWS, LANES), (ROWS, WIDTH)
    dma = pltpu.SemaphoreType.DMA
    far = permute(doc_hidden, [(far_source[i], i) for i in devices])
    qn, dn, gain_line, s_own, *state, picked = call(
        own_kernel,
        [held(block, bf16)] * 2
        + [held((1, WIDTH), f32)]
        + [held(square, f32)] * 3
        + [held(block, f32), held(block, bf16)],
        (),
        distant=(leave(query_hidden), leave(doc_hidden), leave(gain), leave(positives)),
        scratch=[
            pltpu.VMEM(block, bf16), pltpu.VMEM(block, bf16), pltpu.VMEM((GAIN_ROWS, LANES), f32),
            pltpu.VMEM((1, ROWS), jnp.int32), dma((4,)),
        ],
    )
    qn, gain_line, picked, s_own = kept(qn), kept(gain_line), kept(picked), kept(s_own)
    back = permute(dn, [(back_source[i], i) for i in devices])
    swap = permute(dn, swap_route)

    far = call(head_kernel, held(block, bf16), (far, gain_line))
    relay = permute(far, swap_route)
    s_swap, s_far, *state = call(
        functools.partial(pair_kernel, (1, 2)),
        [held(square, f32)] * 4 + [held(block, f32)],
        (swap, far, qn, *map(kept, state)),
        scalars=(neg_blocks,),
        aliases={4: 2, 5: 3, 6: 4},
    )
    s_back = call(
        functools.partial(score_kernel, -2), held(square, f32), (back, qn), scalars=(neg_blocks,), after=(s_far,)
    )
    sizes = [lax.axis_size(a) for a in AXES]
    share = (SUM_ROWS, LANES)
    s_relay, lse, gq, hot, part = call(
        functools.partial(last_kernel, -1),
        [held(square, f32)] * 2 + [held(block, f32), held(square, f32), held((sizes[0], *share), f32)],
        (relay, back, kept(s_back), qn, *map(kept, state), picked, s_own),
        scalars=(neg_blocks,),
        distant=(leave(positives), leave(query_hidden)),
        scratch=[pltpu.VMEM(block, bf16), pltpu.VMEM((1, ROWS), jnp.int32), pltpu.VMEM(share, f32), dma((2,))],
        aliases={7: 2},
    )

    def exchange(x, axis):
        return kept(lax.all_to_all(x, AXES[axis], 0, 0, tiled=True))

    def summed(x, axis):
        return call(sum_kernel, held((sizes[axis], *share), f32), (x,))

    t_near, t_back, t_far, t_own, grad_query = call(
        term_kernel,
        [distant_array((2, *block), bf16)] + [distant_array(block, bf16)] * 4,
        (qn, gain_line, kept(gq), kept(lse), kept(hot), s_own, kept(s_swap), kept(s_relay), kept(s_far), kept(s_back)),
        distant=(leave(query_hidden),),
        scratch=[
            pltpu.VMEM(block, bf16), pltpu.VMEM(block, bf16), pltpu.VMEM((5 * ROWS, ROWS), bf16),
            pltpu.VMEM((5, *block), bf16), pltpu.VMEM((STEP, WIDTH), f32), dma((6,)), dma((PARTS,)),
        ],
        flops=TERM_FLOPS,
    )
    near_term = permute(t_near, swap_route)
    back_term = permute(t_back, [(i, back_source[i]) for i in devices])
    part = summed(exchange(part, 0), 1)
    far_sum = call(
        add_kernel,
        distant_array(block, bf16),
        (),
        distant=(leave(t_far), near_term),
        after=(part,),
        scratch=[pltpu.VMEM((2, *block), bf16), pltpu.VMEM(block, bf16), dma((3, PARTS))],
        flops=ADD_FLOPS,
    )
    far_term = permute(far_sum, [(i, far_source[i]) for i in devices])
    part = summed(exchange(part, 1), 2)
    part = exchange(part, 2)
    grad_doc = call(
        grad_doc_kernel,
        distant_array(block, bf16),
        (gain_line,),
        distant=(leave(doc_hidden), leave(t_own), near_term, back_term, far_term),
        scratch=[
            pltpu.VMEM((5, *block), bf16), pltpu.VMEM(block, bf16), pltpu.VMEM((STEP, WIDTH), f32), dma((6, PARTS))
        ],
        flops=GRAD_FLOPS,
    )
    grad_gain, mean_loss = call(
        functools.partial(end_kernel, float(ROWS * count)),
        [jax.ShapeDtypeStruct((GAIN_ROWS, LANES), f32), jax.ShapeDtypeStruct((1, 1), f32)],
        (part,),
    )
    return mean_loss.reshape(()), grad_gain.reshape(WIDTH), grad_query, grad_doc


def grid_of(count):
    return (8, 12, 8) if count == 768 else (2, count // 16, 8)


def solution(mesh):
    devices = np.asarray(mesh.devices)
    inner = Mesh(devices.reshape(grid_of(devices.size)), AXES)
    placed = (P(AXES, None), P(AXES, None), P(), P(AXES), P(AXES, None))
    return jax.shard_map(
        body,
        mesh=inner,
        in_specs=placed,
        out_specs=(P(), P(), P(AXES, None), P(AXES, None)),
        check_vma=False,
    )
```

```python
import functools
import math

import jax
import jax.numpy as jnp
import numpy as np
from jax import lax
from jax.experimental import pallas as pl
from jax.experimental.pallas import tpu as pltpu
from jax.sharding import Mesh
from jax.sharding import PartitionSpec as P

logit_scale = 4.0
ROWS = 128
WIDTH = 3584
FACTOR = logit_scale / math.sqrt(WIDTH)
LANES = 128
GAIN_ROWS = WIDTH // LANES
SUM_ROWS = 32
CHUNK = 512
HIDDEN = -1e30
STEP = 16
PARTS = 4
PART = ROWS // PARTS
f32, bf16 = jnp.float32, jnp.bfloat16
AXES = ("y", "z", "row")

in_vmem = pl.BlockSpec(memory_space=pltpu.VMEM)
anywhere = pl.BlockSpec(memory_space=pl.ANY)
in_smem = pl.BlockSpec(memory_space=pltpu.SMEM)


def held(shape, dtype):
    return pltpu.VMEM(shape, dtype)


def call(kernel, out_shape, args, scratch=(), aliases=None, scalars=(), distant=(), after=()):
    given = len(scalars) + len(args) + len(distant)

    def run(*refs):
        kernel(*refs[:given], *refs[given + len(after) :])

    flat, tree = jax.tree.flatten(out_shape)
    outs = [anywhere if is_distant(x) else in_vmem for x in flat]
    return pl.pallas_call(
        run,
        in_specs=[in_smem] * len(scalars) + [in_vmem] * len(args) + [anywhere] * (len(distant) + len(after)),
        out_specs=jax.tree.unflatten(tree, outs),
        out_shape=out_shape,
        scratch_shapes=list(scratch),
        input_output_aliases=aliases or {},
        cost_estimate=pl.CostEstimate(flops=1000, bytes_accessed=1000, transcendentals=0),
        compiler_params=pltpu.CompilerParams(vmem_limit_bytes=15 * 2**20),
    )(*scalars, *args, *distant, *after)


def kept(x):
    return pltpu.with_memory_space_constraint(x, pltpu.VMEM)


def leave(x):
    return pltpu.with_memory_space_constraint(x, pltpu.HBM)


def distant_array(shape, dtype):
    return pltpu.HBM(shape, dtype)


def is_distant(shape):
    return getattr(shape, "memory_space", None) == pltpu.HBM


def factor_of(values):
    return lax.rsqrt(jnp.mean(values * values, axis=-1, keepdims=True) + 1e-06)


def head_into(hidden_ref, gain, out_ref):
    for i in range(0, ROWS, STEP):
        values = hidden_ref[i : i + STEP, :].astype(f32)
        out_ref[i : i + STEP, :] = (values * factor_of(values) * gain).astype(bf16)


def scores_of(queries, docs):
    dims = (((1,), (1,)), ((), ()))
    return FACTOR * lax.dot_general(queries, docs, dims, preferred_element_type=f32)


def across(column):
    return jnp.broadcast_to(column, (ROWS, LANES))


def onehot_of(positives_ref):
    slots = lax.broadcasted_iota(jnp.int32, (ROWS, ROWS), 0)
    return (slots == positives_ref[...]).astype(f32).T


def listed(neg_ref, distance):
    place, count = 0, 1
    for axis in AXES:
        place = place * lax.axis_size(axis) + lax.axis_index(axis)
        count = count * lax.axis_size(axis)
    sign = 1 - 2 * lax.rem(place, 2)
    block = lax.rem(place + sign * distance + count, count)
    found = neg_ref[0, 0] == block
    for i in range(1, neg_ref.shape[1]):
        found = jnp.logical_or(found, neg_ref[0, i] == block)
    return found


def own_kernel(
    q_hbm, d_hbm, gain_hbm, pos_hbm,
    qn_ref, dn_ref, gain_ref, s_ref, top_ref, total_ref, acc_ref, picked_ref,
    q_ref, d_ref, line_ref, pos_ref, sems,
):
    pairs = ((d_hbm, d_ref), (gain_hbm, line_ref), (q_hbm, q_ref), (pos_hbm, pos_ref))
    copies = [pltpu.make_async_copy(src, dst, sems.at[i]) for i, (src, dst) in enumerate(pairs)]
    for copy in copies:
        copy.start()
    copies[0].wait()
    copies[1].wait()
    gain = jnp.concatenate([line_ref[i : i + 1, :] for i in range(GAIN_ROWS)], axis=1)
    gain_ref[...] = gain
    head_into(d_ref, gain, dn_ref)
    copies[2].wait()
    copies[3].wait()
    head_into(q_ref, gain, qn_ref)
    scores = scores_of(qn_ref[...], dn_ref[...])
    top = jnp.max(scores, axis=1, keepdims=True)
    probs = jnp.exp(scores - top)
    s_ref[...] = scores
    top_ref[...] = across(top)
    total_ref[...] = across(jnp.sum(probs, axis=1, keepdims=True))
    probs = probs.astype(bf16)
    onehot = onehot_of(pos_ref).astype(bf16)
    for c in range(0, WIDTH, CHUNK):
        docs = dn_ref[:, c : c + CHUNK]
        acc_ref[:, c : c + CHUNK] = jnp.dot(probs, docs, preferred_element_type=f32)
        picked_ref[:, c : c + CHUNK] = jnp.dot(onehot, docs, preferred_element_type=f32).astype(bf16)


def head_kernel(x_ref, gain_ref, out_ref):
    head_into(x_ref, gain_ref[...], out_ref)


def fold(blocks, top0_ref, total0_ref):
    before = top0_ref[:, 0:1]
    top = before
    for scores in blocks:
        top = jnp.maximum(top, jnp.max(scores, axis=1, keepdims=True))
    shrink = jnp.exp(before - top)
    total = total0_ref[:, 0:1] * shrink
    probs = []
    for scores in blocks:
        prob = jnp.exp(scores - top)
        total = total + jnp.sum(prob, axis=1, keepdims=True)
        probs.append(prob.astype(bf16))
    return top, total, shrink, probs


def pair_kernel(
    distances, neg_ref, swap_ref, far_ref, qn_ref, top0_ref, total0_ref, acc0_ref,
    s_swap_ref, s_far_ref, top_ref, total_ref, acc_ref,
):
    for distance, dn_ref, s_ref in zip(distances, (swap_ref, far_ref), (s_swap_ref, s_far_ref)):
        s_ref[...] = jnp.where(listed(neg_ref, distance), scores_of(qn_ref[...], dn_ref[...]), HIDDEN)
    top, total, shrink, probs = fold((s_swap_ref[...], s_far_ref[...]), top0_ref, total0_ref)
    for c in range(0, WIDTH, CHUNK):
        cols = slice(c, c + CHUNK)
        term = jnp.dot(probs[0], swap_ref[:, cols], preferred_element_type=f32)
        term = term + jnp.dot(probs[1], far_ref[:, cols], preferred_element_type=f32)
        acc_ref[:, cols] = acc0_ref[:, cols] * shrink + term
    top_ref[...] = across(top)
    total_ref[...] = across(total)


def score_kernel(distance, neg_ref, dn_ref, qn_ref, s_ref):
    s_ref[...] = jnp.where(listed(neg_ref, distance), scores_of(qn_ref[...], dn_ref[...]), HIDDEN)


def last_kernel(
    distance, neg_ref, dn_ref, back_ref, s_back_ref, qn_ref, top0_ref, total0_ref, acc0_ref, picked_ref, s_own_ref,
    pos_hbm, q_hbm,
    s_ref, lse_ref, gq_ref, hot_ref, lines, q_ref, pos_ref, sems,
):
    copies = [pltpu.make_async_copy(q_hbm, q_ref, sems.at[0]), pltpu.make_async_copy(pos_hbm, pos_ref, sems.at[1])]
    for copy in copies:
        copy.start()
    scores = jnp.where(listed(neg_ref, distance), scores_of(qn_ref[...], dn_ref[...]), HIDDEN)
    top, total, shrink, (probs, back_probs) = fold((scores, s_back_ref[...]), top0_ref, total0_ref)
    lse = top + jnp.log(total)
    s_ref[...] = scores
    lse_ref[...] = across(lse)
    for copy in copies:
        copy.wait()
    onehot = onehot_of(pos_ref)
    hot_ref[...] = onehot
    loss = jnp.sum(lse - jnp.sum(s_own_ref[...] * onehot, axis=1, keepdims=True))
    share = FACTOR / total
    kept_share = shrink * share
    squares = [
        jnp.sum(jnp.square(q_ref[i : i + STEP, :].astype(f32)), axis=-1, keepdims=True) for i in range(0, ROWS, STEP)
    ]
    factor = lax.rsqrt(jnp.concatenate(squares, axis=0) / WIDTH + 1e-06)
    for c in range(0, WIDTH, CHUNK):
        cols = slice(c, c + CHUNK)
        term = jnp.dot(probs, dn_ref[:, cols], preferred_element_type=f32)
        term = term + jnp.dot(back_probs, back_ref[:, cols], preferred_element_type=f32)
        gq = acc0_ref[:, cols] * kept_share + term * share - FACTOR * picked_ref[:, cols].astype(f32)
        gq_ref[:, cols] = gq
        added = 2.0 * jnp.sum(gq * (q_ref[:, cols].astype(f32) * factor), axis=0, keepdims=True)
        for i in range(0, CHUNK, LANES):
            lines[(c + i) // LANES : (c + i) // LANES + 1, :] = added[:, i : i + LANES]
    lines[GAIN_ROWS:, :] = jnp.full((SUM_ROWS - GAIN_ROWS, LANES), loss, f32)


def turned(block_ref, lse_ref, hot_ref=None):
    weight = jnp.exp(block_ref[...] - lse_ref[...])
    if hot_ref is not None:
        weight = weight - hot_ref[...]
    return weight.T.astype(bf16)


def near_kernel(qn_ref, lse_ref, s_relay_ref, s_swap_ref, lines_ref, near_ref, part_ref):
    weights = [turned(block_ref, lse_ref) for block_ref in (s_relay_ref, s_swap_ref)]
    for c in range(0, WIDTH, CHUNK):
        cols = slice(c, c + CHUNK)
        for k, weight in enumerate(weights):
            near_ref[k, :, cols] = jnp.dot(weight, qn_ref[:, cols], preferred_element_type=f32).astype(bf16)
    part_ref[...] = jnp.broadcast_to(lines_ref[...][None], part_ref.shape)


def far_kernel(qn_ref, lse_ref, s_back_ref, s_far_ref, near_ref, back_ref, far_ref):
    w_back, w_far = (turned(block_ref, lse_ref) for block_ref in (s_back_ref, s_far_ref))
    for c in range(0, WIDTH, CHUNK):
        cols = slice(c, c + CHUNK)
        queries = qn_ref[:, cols]
        back_ref[:, cols] = jnp.dot(w_back, queries, preferred_element_type=f32).astype(bf16)
        term = jnp.dot(w_far, queries, preferred_element_type=f32)
        far_ref[:, cols] = (term + near_ref[0, :, cols].astype(f32)).astype(bf16)


def home_kernel(
    qn_ref, lse_ref, s_own_ref, hot_ref, near_ref, gain_ref, gq_ref, q_hbm, own_ref, grad_hbm, q_ref, grad_ref, scaled_ref, sems
):
    incoming = pltpu.make_async_copy(q_hbm, q_ref, sems.at[PARTS])
    incoming.start()
    weight = turned(s_own_ref, lse_ref, hot_ref)
    for c in range(0, WIDTH, CHUNK):
        cols = slice(c, c + CHUNK)
        term = jnp.dot(weight, qn_ref[:, cols], preferred_element_type=f32)
        own_ref[:, cols] = term + near_ref[1, :, cols].astype(f32)
    incoming.wait()

    def values_at(rows, cols):
        return q_ref[rows, cols].astype(f32)

    def cotangent_at(rows, cols):
        return gq_ref[rows, cols]

    send_parts(lambda rows: pull(values_at, cotangent_at, gain_ref, scaled_ref, grad_ref, rows), grad_ref, grad_hbm, sems)


def grad_doc_kernel(gain_ref, own_ref, back_ref, far_ref, d_hbm, grad_hbm, d_ref, grad_ref, scaled_ref, sems, in_sems):
    incoming = []
    for part in range(PARTS):
        rows = pl.ds(part * PART, PART)
        copy = pltpu.make_async_copy(d_hbm.at[rows, :], d_ref.at[rows, :], in_sems.at[part])
        copy.start()
        incoming.append(copy)

    def values_at(rows, cols):
        return d_ref[rows, cols].astype(f32)

    def cotangent_at(rows, cols):
        total = own_ref[rows, cols] + back_ref[rows, cols].astype(f32) + far_ref[rows, cols].astype(f32)
        return FACTOR * total

    def work(rows):
        if rows.start % PART == 0:
            incoming[rows.start // PART].wait()
        pull(values_at, cotangent_at, gain_ref, scaled_ref, grad_ref, rows)

    send_parts(work, grad_ref, grad_hbm, sems)


def send_parts(work, out_ref, target, sems):
    outgoing = []
    for part in range(PARTS):
        for i in range(part * PART, (part + 1) * PART, STEP):
            work(slice(i, i + STEP))
        rows = pl.ds(part * PART, PART)
        copy = pltpu.make_async_copy(out_ref.at[rows, :], target.at[rows, :], sems.at[part])
        copy.start()
        outgoing.append(copy)
    for copy in outgoing:
        copy.wait()


def pull(values_at, cotangent_at, gain_ref, scaled_ref, out_ref, rows):
    square = jnp.zeros((STEP, CHUNK), f32)
    inner = jnp.zeros((STEP, CHUNK), f32)
    chunks = [slice(c, c + CHUNK) for c in range(0, WIDTH, CHUNK)]
    for cols in chunks:
        values = values_at(rows, cols)
        scaled = gain_ref[:, cols] * cotangent_at(rows, cols)
        scaled_ref[:, cols] = scaled
        square = square + values * values
        inner = inner + values * scaled
    factor = lax.rsqrt(jnp.sum(square, axis=-1, keepdims=True) / WIDTH + 1e-06)
    inner = factor * factor * factor * (jnp.sum(inner, axis=-1, keepdims=True) / WIDTH)
    for cols in chunks:
        grad = factor * scaled_ref[:, cols] - values_at(rows, cols) * inner
        out_ref[rows, cols] = grad.astype(bf16)


def sum_kernel(in_ref, out_ref):
    total = jnp.sum(in_ref[...], axis=0)
    out_ref[...] = jnp.broadcast_to(total[None], out_ref.shape)


def end_kernel(denom, in_ref, gain_ref, loss_ref):
    total = jnp.sum(in_ref[...], axis=0) / denom
    gain_ref[...] = total[:GAIN_ROWS]
    loss_ref[...] = total[GAIN_ROWS : GAIN_ROWS + 1, 0:1]


def body(query_hidden, doc_hidden, gain, positives, neg_blocks):
    count = lax.axis_size(AXES)
    gain = gain.reshape(GAIN_ROWS, LANES)
    positives = positives.reshape(1, ROWS)

    devices = range(count)
    far_source = [(i + 2 if i % 2 == 0 else i - 2) % count for i in devices]
    back_source = [(i - 2 if i % 2 == 0 else i + 2) % count for i in devices]

    def permute(x, route):
        return lax.ppermute(x, AXES, route)

    swap_route = [(i, i ^ 1) for i in devices]
    square, block = (ROWS, LANES), (ROWS, WIDTH)
    dma = pltpu.SemaphoreType.DMA
    far = permute(doc_hidden, [(far_source[i], i) for i in devices])
    qn, dn, gain_line, s_own, *state, picked = call(
        own_kernel,
        [held(block, bf16)] * 2
        + [held((1, WIDTH), f32)]
        + [held(square, f32)] * 3
        + [held(block, f32), held(block, bf16)],
        (),
        distant=(leave(query_hidden), leave(doc_hidden), leave(gain), leave(positives)),
        scratch=[
            pltpu.VMEM(block, bf16), pltpu.VMEM(block, bf16), pltpu.VMEM((GAIN_ROWS, LANES), f32),
            pltpu.VMEM((1, ROWS), jnp.int32), dma((4,)),
        ],
    )
    qn, gain_line, picked, s_own = kept(qn), kept(gain_line), kept(picked), kept(s_own)
    back = permute(dn, [(back_source[i], i) for i in devices])
    swap = permute(dn, swap_route)

    far = call(head_kernel, held(block, bf16), (far, gain_line))
    relay = permute(far, swap_route)
    s_swap, s_far, *state = call(
        functools.partial(pair_kernel, (1, 2)),
        [held(square, f32)] * 4 + [held(block, f32)],
        (swap, far, qn, *map(kept, state)),
        scalars=(neg_blocks,),
        aliases={4: 2, 5: 3, 6: 4},
    )
    s_back = call(
        functools.partial(score_kernel, -2), held(square, f32), (back, qn), scalars=(neg_blocks,), after=(s_far,)
    )
    sizes = [lax.axis_size(a) for a in AXES]
    share = (SUM_ROWS, LANES)
    s_relay, lse, gq, hot, lines = call(
        functools.partial(last_kernel, -1),
        [held(square, f32)] * 2 + [held(block, f32), held(square, f32), held(share, f32)],
        (relay, back, kept(s_back), qn, *map(kept, state), picked, s_own),
        scalars=(neg_blocks,),
        distant=(leave(positives), leave(query_hidden)),
        scratch=[pltpu.VMEM(block, bf16), pltpu.VMEM((1, ROWS), jnp.int32), dma((2,))],
        aliases={7: 2},
    )
    lse = kept(lse)

    def exchange(x, axis):
        return kept(lax.all_to_all(x, AXES[axis], 0, 0, tiled=True))

    def summed(x, axis):
        return call(sum_kernel, held((sizes[axis], *share), f32), (x,))

    t_near, part = call(
        near_kernel,
        [held((2, *block), bf16), held((sizes[1], *share), f32)],
        (qn, lse, kept(s_relay), kept(s_swap), kept(lines)),
    )
    near_term = permute(t_near, swap_route)
    part = summed(exchange(part, 1), 0)
    t_back, far_sum = call(
        far_kernel, [held(block, bf16)] * 2, (qn, lse, kept(s_back), kept(s_far), near_term), after=(part,)
    )
    far_term = permute(far_sum, [(i, far_source[i]) for i in devices])
    back_term = permute(t_back, [(i, back_source[i]) for i in devices])
    t_own, grad_query = call(
        home_kernel,
        [held(block, f32), distant_array(block, bf16)],
        (qn, lse, s_own, kept(hot), near_term, gain_line, kept(gq)),
        distant=(leave(query_hidden),),
        scratch=[pltpu.VMEM(block, bf16), pltpu.VMEM(block, bf16), pltpu.VMEM((STEP, WIDTH), f32), dma((PARTS + 1,))],
    )
    part = summed(exchange(part, 0), 2)
    part = exchange(part, 2)
    grad_doc = call(
        grad_doc_kernel,
        distant_array(block, bf16),
        (gain_line, kept(t_own), back_term, far_term),
        distant=(leave(doc_hidden),),
        scratch=[
            pltpu.VMEM(block, bf16), pltpu.VMEM(block, bf16), pltpu.VMEM((STEP, WIDTH), f32), dma((PARTS,)), dma((PARTS,))
        ],
    )
    grad_gain, mean_loss = call(
        functools.partial(end_kernel, float(ROWS * count)),
        [jax.ShapeDtypeStruct((GAIN_ROWS, LANES), f32), jax.ShapeDtypeStruct((1, 1), f32)],
        (part,),
    )
    return mean_loss.reshape(()), grad_gain.reshape(WIDTH), grad_query, grad_doc


def grid_of(count):
    return (8, 12, 8) if count == 768 else (2, count // 16, 8)


def solution(mesh):
    devices = np.asarray(mesh.devices)
    inner = Mesh(devices.reshape(grid_of(devices.size)), AXES)
    placed = (P(AXES, None), P(AXES, None), P(), P(AXES), P(AXES, None))
    return jax.shard_map(
        body,
        mesh=inner,
        in_specs=placed,
        out_specs=(P(), P(), P(AXES, None), P(AXES, None)),
        check_vma=False,
    )
```

```python
import functools
import math

import jax
import jax.numpy as jnp
import numpy as np
from jax import lax
from jax.experimental import pallas as pl
from jax.experimental.pallas import tpu as pltpu
from jax.sharding import Mesh
from jax.sharding import PartitionSpec as P

logit_scale = 4.0
ROWS = 128
WIDTH = 3584
FACTOR = logit_scale / math.sqrt(WIDTH)
LANES = 128
GAIN_ROWS = WIDTH // LANES
SUM_ROWS = 32
CHUNK = 512
HIDDEN = -1e30
STEP = 16
PARTS = 4
PART = ROWS // PARTS
f32, bf16 = jnp.float32, jnp.bfloat16
AXES = ("y", "z", "row")

in_vmem = pl.BlockSpec(memory_space=pltpu.VMEM)
anywhere = pl.BlockSpec(memory_space=pl.ANY)
in_smem = pl.BlockSpec(memory_space=pltpu.SMEM)


def held(shape, dtype):
    return pltpu.VMEM(shape, dtype)


def call(kernel, out_shape, args, scratch=(), aliases=None, scalars=(), distant=(), after=()):
    given = len(scalars) + len(args) + len(distant)

    def run(*refs):
        kernel(*refs[:given], *refs[given + len(after) :])

    flat, tree = jax.tree.flatten(out_shape)
    outs = [anywhere if is_distant(x) else in_vmem for x in flat]
    return pl.pallas_call(
        run,
        in_specs=[in_smem] * len(scalars) + [in_vmem] * len(args) + [anywhere] * (len(distant) + len(after)),
        out_specs=jax.tree.unflatten(tree, outs),
        out_shape=out_shape,
        scratch_shapes=list(scratch),
        input_output_aliases=aliases or {},
        cost_estimate=pl.CostEstimate(flops=1000, bytes_accessed=1000, transcendentals=0),
        compiler_params=pltpu.CompilerParams(vmem_limit_bytes=15 * 2**20),
    )(*scalars, *args, *distant, *after)


def kept(x):
    return pltpu.with_memory_space_constraint(x, pltpu.VMEM)


def leave(x):
    return pltpu.with_memory_space_constraint(x, pltpu.HBM)


def distant_array(shape, dtype):
    return pltpu.HBM(shape, dtype)


def is_distant(shape):
    return getattr(shape, "memory_space", None) == pltpu.HBM


def factor_of(values):
    return lax.rsqrt(jnp.mean(values * values, axis=-1, keepdims=True) + 1e-06)


def head_into(hidden_ref, gain, out_ref, first=0, rows=ROWS):
    for i in range(first, first + rows, STEP):
        values = hidden_ref[i : i + STEP, :].astype(f32)
        out_ref[i : i + STEP, :] = (values * factor_of(values) * gain).astype(bf16)


def scores_of(queries, docs):
    dims = (((1,), (1,)), ((), ()))
    return FACTOR * lax.dot_general(queries, docs, dims, preferred_element_type=f32)


def across(column):
    return jnp.broadcast_to(column, (ROWS, LANES))


def onehot_of(positives_ref):
    slots = lax.broadcasted_iota(jnp.int32, (ROWS, ROWS), 0)
    return (slots == positives_ref[...]).astype(f32).T


def listed(neg_ref, distance):
    place, count = 0, 1
    for axis in AXES:
        place = place * lax.axis_size(axis) + lax.axis_index(axis)
        count = count * lax.axis_size(axis)
    sign = 1 - 2 * lax.rem(place, 2)
    block = lax.rem(place + sign * distance + count, count)
    found = neg_ref[0, 0] == block
    for i in range(1, neg_ref.shape[1]):
        found = jnp.logical_or(found, neg_ref[0, i] == block)
    return found


def own_kernel(
    q_hbm, d_hbm, gain_hbm, pos_hbm,
    qn_ref, dn_ref, gain_ref, s_ref, top_ref, total_ref, acc_ref, picked_ref,
    q_ref, d_ref, line_ref, pos_ref, sems,
):
    copies = [pltpu.make_async_copy(gain_hbm, line_ref, sems.at[2 * PARTS])]
    for k, (src, dst) in enumerate(((d_hbm, d_ref), (q_hbm, q_ref))):
        for part in range(PARTS):
            rows = pl.ds(part * PART, PART)
            copies.append(pltpu.make_async_copy(src.at[rows, :], dst.at[rows, :], sems.at[k * PARTS + part]))
    copies.append(pltpu.make_async_copy(pos_hbm, pos_ref, sems.at[2 * PARTS + 1]))
    for copy in copies:
        copy.start()
    copies[0].wait()
    gain = jnp.concatenate([line_ref[i : i + 1, :] for i in range(GAIN_ROWS)], axis=1)
    gain_ref[...] = gain
    for k, (hidden_ref, out_ref) in enumerate(((d_ref, dn_ref), (q_ref, qn_ref))):
        for part in range(PARTS):
            copies[1 + k * PARTS + part].wait()
            head_into(hidden_ref, gain, out_ref, part * PART, PART)
    copies[-1].wait()
    scores = scores_of(qn_ref[...], dn_ref[...])
    top = jnp.max(scores, axis=1, keepdims=True)
    probs = jnp.exp(scores - top)
    s_ref[...] = scores
    top_ref[...] = across(top)
    total_ref[...] = across(jnp.sum(probs, axis=1, keepdims=True))
    probs = probs.astype(bf16)
    onehot = onehot_of(pos_ref).astype(bf16)
    for c in range(0, WIDTH, CHUNK):
        docs = dn_ref[:, c : c + CHUNK]
        acc_ref[:, c : c + CHUNK] = jnp.dot(probs, docs, preferred_element_type=f32)
        picked_ref[:, c : c + CHUNK] = jnp.dot(onehot, docs, preferred_element_type=f32).astype(bf16)


def head_kernel(x_ref, gain_ref, out_ref):
    head_into(x_ref, gain_ref[...], out_ref)


def fold(blocks, top0_ref, total0_ref):
    before = top0_ref[:, 0:1]
    top = before
    for scores in blocks:
        top = jnp.maximum(top, jnp.max(scores, axis=1, keepdims=True))
    shrink = jnp.exp(before - top)
    total = total0_ref[:, 0:1] * shrink
    probs = []
    for scores in blocks:
        prob = jnp.exp(scores - top)
        total = total + jnp.sum(prob, axis=1, keepdims=True)
        probs.append(prob.astype(bf16))
    return top, total, shrink, probs


def pair_kernel(
    distances, neg_ref, swap_ref, far_ref, qn_ref, top0_ref, total0_ref, acc0_ref,
    s_swap_ref, s_far_ref, top_ref, total_ref, acc_ref,
):
    for distance, dn_ref, s_ref in zip(distances, (swap_ref, far_ref), (s_swap_ref, s_far_ref)):
        s_ref[...] = jnp.where(listed(neg_ref, distance), scores_of(qn_ref[...], dn_ref[...]), HIDDEN)
    top, total, shrink, probs = fold((s_swap_ref[...], s_far_ref[...]), top0_ref, total0_ref)
    for c in range(0, WIDTH, CHUNK):
        cols = slice(c, c + CHUNK)
        term = jnp.dot(probs[0], swap_ref[:, cols], preferred_element_type=f32)
        term = term + jnp.dot(probs[1], far_ref[:, cols], preferred_element_type=f32)
        acc_ref[:, cols] = acc0_ref[:, cols] * shrink + term
    top_ref[...] = across(top)
    total_ref[...] = across(total)


def score_kernel(distance, neg_ref, dn_ref, qn_ref, s_ref):
    s_ref[...] = jnp.where(listed(neg_ref, distance), scores_of(qn_ref[...], dn_ref[...]), HIDDEN)


def last_kernel(
    distance, neg_ref, dn_ref, back_ref, s_back_ref, qn_ref, top0_ref, total0_ref, acc0_ref, picked_ref, s_own_ref,
    pos_hbm, q_hbm,
    s_ref, lse_ref, gq_ref, hot_ref, lines, q_ref, pos_ref, sems,
):
    copies = [pltpu.make_async_copy(q_hbm, q_ref, sems.at[0]), pltpu.make_async_copy(pos_hbm, pos_ref, sems.at[1])]
    for copy in copies:
        copy.start()
    scores = jnp.where(listed(neg_ref, distance), scores_of(qn_ref[...], dn_ref[...]), HIDDEN)
    top, total, shrink, (probs, back_probs) = fold((scores, s_back_ref[...]), top0_ref, total0_ref)
    lse = top + jnp.log(total)
    s_ref[...] = scores
    lse_ref[...] = across(lse)
    for copy in copies:
        copy.wait()
    onehot = onehot_of(pos_ref)
    hot_ref[...] = onehot
    loss = jnp.sum(lse - jnp.sum(s_own_ref[...] * onehot, axis=1, keepdims=True))
    share = FACTOR / total
    kept_share = shrink * share
    squares = [
        jnp.sum(jnp.square(q_ref[i : i + STEP, :].astype(f32)), axis=-1, keepdims=True) for i in range(0, ROWS, STEP)
    ]
    factor = lax.rsqrt(jnp.concatenate(squares, axis=0) / WIDTH + 1e-06)
    for c in range(0, WIDTH, CHUNK):
        cols = slice(c, c + CHUNK)
        term = jnp.dot(probs, dn_ref[:, cols], preferred_element_type=f32)
        term = term + jnp.dot(back_probs, back_ref[:, cols], preferred_element_type=f32)
        gq = acc0_ref[:, cols] * kept_share + term * share - FACTOR * picked_ref[:, cols].astype(f32)
        gq_ref[:, cols] = gq
        added = 2.0 * jnp.sum(gq * (q_ref[:, cols].astype(f32) * factor), axis=0, keepdims=True)
        for i in range(0, CHUNK, LANES):
            lines[(c + i) // LANES : (c + i) // LANES + 1, :] = added[:, i : i + LANES]
    lines[GAIN_ROWS:, :] = jnp.full((SUM_ROWS - GAIN_ROWS, LANES), loss, f32)


def turned(block_ref, lse_ref, hot_ref=None):
    weight = jnp.exp(block_ref[...] - lse_ref[...])
    if hot_ref is not None:
        weight = weight - hot_ref[...]
    return weight.T.astype(bf16)


def near_kernel(qn_ref, lse_ref, s_relay_ref, s_swap_ref, s_back_ref, lines_ref, near_ref, back_ref, part_ref):
    w_relay, w_swap, w_back = (turned(block_ref, lse_ref) for block_ref in (s_relay_ref, s_swap_ref, s_back_ref))
    for c in range(0, WIDTH, CHUNK):
        cols = slice(c, c + CHUNK)
        queries = qn_ref[:, cols]
        near_ref[0, :, cols] = jnp.dot(w_relay, queries, preferred_element_type=f32).astype(bf16)
        near_ref[1, :, cols] = jnp.dot(w_swap, queries, preferred_element_type=f32).astype(bf16)
        back_ref[:, cols] = jnp.dot(w_back, queries, preferred_element_type=f32).astype(bf16)
    part_ref[...] = jnp.broadcast_to(lines_ref[...][None], part_ref.shape)


def far_kernel(qn_ref, lse_ref, s_far_ref, near_ref, far_ref):
    weight = turned(s_far_ref, lse_ref)
    for c in range(0, WIDTH, CHUNK):
        cols = slice(c, c + CHUNK)
        term = jnp.dot(weight, qn_ref[:, cols], preferred_element_type=f32)
        far_ref[:, cols] = (term + near_ref[0, :, cols].astype(f32)).astype(bf16)


def home_kernel(
    qn_ref, lse_ref, s_own_ref, hot_ref, near_ref, gain_ref, gq_ref, q_hbm, own_ref, grad_hbm, q_ref, grad_ref, scaled_ref, sems
):
    incoming = pltpu.make_async_copy(q_hbm, q_ref, sems.at[PARTS])
    incoming.start()
    weight = turned(s_own_ref, lse_ref, hot_ref)
    for c in range(0, WIDTH, CHUNK):
        cols = slice(c, c + CHUNK)
        term = jnp.dot(weight, qn_ref[:, cols], preferred_element_type=f32)
        own_ref[:, cols] = term + near_ref[1, :, cols].astype(f32)
    incoming.wait()

    def values_at(rows, cols):
        return q_ref[rows, cols].astype(f32)

    def cotangent_at(rows, cols):
        return gq_ref[rows, cols]

    send_parts(lambda rows: pull(values_at, cotangent_at, gain_ref, scaled_ref, grad_ref, rows), grad_ref, grad_hbm, sems)


def grad_doc_kernel(gain_ref, own_ref, back_ref, far_ref, d_hbm, grad_hbm, d_ref, grad_ref, scaled_ref, sems, in_sems):
    incoming = []
    for part in range(PARTS):
        rows = pl.ds(part * PART, PART)
        copy = pltpu.make_async_copy(d_hbm.at[rows, :], d_ref.at[rows, :], in_sems.at[part])
        copy.start()
        incoming.append(copy)

    def values_at(rows, cols):
        return d_ref[rows, cols].astype(f32)

    def cotangent_at(rows, cols):
        total = own_ref[rows, cols] + back_ref[rows, cols].astype(f32) + far_ref[rows, cols].astype(f32)
        return FACTOR * total

    def work(rows):
        if rows.start % PART == 0:
            incoming[rows.start // PART].wait()
        pull(values_at, cotangent_at, gain_ref, scaled_ref, grad_ref, rows)

    send_parts(work, grad_ref, grad_hbm, sems)


def send_parts(work, out_ref, target, sems):
    outgoing = []
    for part in range(PARTS):
        for i in range(part * PART, (part + 1) * PART, STEP):
            work(slice(i, i + STEP))
        rows = pl.ds(part * PART, PART)
        copy = pltpu.make_async_copy(out_ref.at[rows, :], target.at[rows, :], sems.at[part])
        copy.start()
        outgoing.append(copy)
    for copy in outgoing:
        copy.wait()


def pull(values_at, cotangent_at, gain_ref, scaled_ref, out_ref, rows):
    square = jnp.zeros((STEP, CHUNK), f32)
    inner = jnp.zeros((STEP, CHUNK), f32)
    chunks = [slice(c, c + CHUNK) for c in range(0, WIDTH, CHUNK)]
    for cols in chunks:
        values = values_at(rows, cols)
        scaled = gain_ref[:, cols] * cotangent_at(rows, cols)
        scaled_ref[:, cols] = scaled
        square = square + values * values
        inner = inner + values * scaled
    factor = lax.rsqrt(jnp.sum(square, axis=-1, keepdims=True) / WIDTH + 1e-06)
    inner = factor * factor * factor * (jnp.sum(inner, axis=-1, keepdims=True) / WIDTH)
    for cols in chunks:
        grad = factor * scaled_ref[:, cols] - values_at(rows, cols) * inner
        out_ref[rows, cols] = grad.astype(bf16)


def sum_kernel(in_ref, out_ref):
    total = jnp.sum(in_ref[...], axis=0)
    out_ref[...] = jnp.broadcast_to(total[None], out_ref.shape)


def end_kernel(denom, in_ref, gain_ref, loss_ref):
    total = jnp.sum(in_ref[...], axis=0) / denom
    gain_ref[...] = total[:GAIN_ROWS]
    loss_ref[...] = total[GAIN_ROWS : GAIN_ROWS + 1, 0:1]


def body(query_hidden, doc_hidden, gain, positives, neg_blocks):
    count = lax.axis_size(AXES)
    gain = gain.reshape(GAIN_ROWS, LANES)
    positives = positives.reshape(1, ROWS)

    devices = range(count)
    far_source = [(i + 2 if i % 2 == 0 else i - 2) % count for i in devices]
    back_source = [(i - 2 if i % 2 == 0 else i + 2) % count for i in devices]

    def permute(x, route):
        return lax.ppermute(x, AXES, route)

    swap_route = [(i, i ^ 1) for i in devices]
    square, block = (ROWS, LANES), (ROWS, WIDTH)
    dma = pltpu.SemaphoreType.DMA
    far = permute(doc_hidden, [(far_source[i], i) for i in devices])
    qn, dn, gain_line, s_own, *state, picked = call(
        own_kernel,
        [held(block, bf16)] * 2
        + [held((1, WIDTH), f32)]
        + [held(square, f32)] * 3
        + [held(block, f32), held(block, bf16)],
        (),
        distant=(leave(query_hidden), leave(doc_hidden), leave(gain), leave(positives)),
        scratch=[
            pltpu.VMEM(block, bf16), pltpu.VMEM(block, bf16), pltpu.VMEM((GAIN_ROWS, LANES), f32),
            pltpu.VMEM((1, ROWS), jnp.int32), dma((2 * PARTS + 2,)),
        ],
    )
    qn, gain_line, picked, s_own = kept(qn), kept(gain_line), kept(picked), kept(s_own)
    back = permute(dn, [(back_source[i], i) for i in devices])
    swap = permute(dn, swap_route)

    far = call(head_kernel, held(block, bf16), (far, gain_line))
    relay = permute(far, swap_route)
    s_swap, s_far, *state = call(
        functools.partial(pair_kernel, (1, 2)),
        [held(square, f32)] * 4 + [held(block, f32)],
        (swap, far, qn, *map(kept, state)),
        scalars=(neg_blocks,),
        aliases={4: 2, 5: 3, 6: 4},
    )
    s_back = call(
        functools.partial(score_kernel, -2), held(square, f32), (back, qn), scalars=(neg_blocks,), after=(s_far,)
    )
    sizes = [lax.axis_size(a) for a in AXES]
    share = (SUM_ROWS, LANES)
    s_relay, lse, gq, hot, lines = call(
        functools.partial(last_kernel, -1),
        [held(square, f32)] * 2 + [held(block, f32), held(square, f32), held(share, f32)],
        (relay, back, kept(s_back), qn, *map(kept, state), picked, s_own),
        scalars=(neg_blocks,),
        distant=(leave(positives), leave(query_hidden)),
        scratch=[pltpu.VMEM(block, bf16), pltpu.VMEM((1, ROWS), jnp.int32), dma((2,))],
        aliases={7: 2},
    )
    lse = kept(lse)

    def exchange(x, axis):
        return kept(lax.all_to_all(x, AXES[axis], 0, 0, tiled=True))

    def summed(x, axis, after=()):
        return call(sum_kernel, held((sizes[axis], *share), f32), (x,), after=after)

    t_near, t_back, part = call(
        near_kernel,
        [held((2, *block), bf16), held(block, bf16), held((sizes[0], *share), f32)],
        (qn, lse, kept(s_relay), kept(s_swap), kept(s_back), kept(lines)),
    )
    near_term = permute(t_near, swap_route)
    back_term = permute(t_back, [(i, back_source[i]) for i in devices])
    part = summed(exchange(part, 0), 1, after=(back_term,))
    far_sum = call(far_kernel, held(block, bf16), (qn, lse, kept(s_far), near_term), after=(part,))
    far_term = permute(far_sum, [(i, far_source[i]) for i in devices])
    t_own, grad_query = call(
        home_kernel,
        [held(block, f32), distant_array(block, bf16)],
        (qn, lse, s_own, kept(hot), near_term, gain_line, kept(gq)),
        distant=(leave(query_hidden),),
        scratch=[pltpu.VMEM(block, bf16), pltpu.VMEM(block, bf16), pltpu.VMEM((STEP, WIDTH), f32), dma((PARTS + 1,))],
    )
    part = summed(exchange(part, 1), 2)
    part = exchange(part, 2)
    grad_doc = call(
        grad_doc_kernel,
        distant_array(block, bf16),
        (gain_line, kept(t_own), back_term, far_term),
        distant=(leave(doc_hidden),),
        scratch=[
            pltpu.VMEM(block, bf16), pltpu.VMEM(block, bf16), pltpu.VMEM((STEP, WIDTH), f32), dma((PARTS,)), dma((PARTS,))
        ],
    )
    grad_gain, mean_loss = call(
        functools.partial(end_kernel, float(ROWS * count)),
        [jax.ShapeDtypeStruct((GAIN_ROWS, LANES), f32), jax.ShapeDtypeStruct((1, 1), f32)],
        (part,),
    )
    return mean_loss.reshape(()), grad_gain.reshape(WIDTH), grad_query, grad_doc


def grid_of(count):
    return (8, 12, 8) if count == 768 else (2, count // 16, 8)


def solution(mesh):
    devices = np.asarray(mesh.devices)
    inner = Mesh(devices.reshape(grid_of(devices.size)), AXES)
    placed = (P(AXES, None), P(AXES, None), P(), P(AXES), P(AXES, None))
    return jax.shard_map(
        body,
        mesh=inner,
        in_specs=placed,
        out_specs=(P(), P(), P(AXES, None), P(AXES, None)),
        check_vma=False,
    )
```

```python
import functools
import math

import jax
import jax.numpy as jnp
import numpy as np
from jax import lax
from jax.experimental import pallas as pl
from jax.experimental.pallas import tpu as pltpu
from jax.sharding import Mesh
from jax.sharding import PartitionSpec as P

logit_scale = 4.0
ROWS = 128
WIDTH = 3584
FACTOR = logit_scale / math.sqrt(WIDTH)
LANES = 128
GAIN_ROWS = WIDTH // LANES
SUM_ROWS = 32
CHUNK = 512
HIDDEN = -1e30
STEP = 16
PARTS = 4
PART = ROWS // PARTS
f32, bf16 = jnp.float32, jnp.bfloat16
AXES = ("y", "z", "row")

in_vmem = pl.BlockSpec(memory_space=pltpu.VMEM)
anywhere = pl.BlockSpec(memory_space=pl.ANY)
in_smem = pl.BlockSpec(memory_space=pltpu.SMEM)


def held(shape, dtype):
    return pltpu.VMEM(shape, dtype)


def call(kernel, out_shape, args, scratch=(), aliases=None, scalars=(), distant=(), after=()):
    given = len(scalars) + len(args) + len(distant)

    def run(*refs):
        kernel(*refs[:given], *refs[given + len(after) :])

    flat, tree = jax.tree.flatten(out_shape)
    outs = [anywhere if is_distant(x) else in_vmem for x in flat]
    return pl.pallas_call(
        run,
        in_specs=[in_smem] * len(scalars) + [in_vmem] * len(args) + [anywhere] * (len(distant) + len(after)),
        out_specs=jax.tree.unflatten(tree, outs),
        out_shape=out_shape,
        scratch_shapes=list(scratch),
        input_output_aliases=aliases or {},
        cost_estimate=pl.CostEstimate(flops=1000, bytes_accessed=1000, transcendentals=0),
        compiler_params=pltpu.CompilerParams(vmem_limit_bytes=15 * 2**20),
    )(*scalars, *args, *distant, *after)


def kept(x):
    return pltpu.with_memory_space_constraint(x, pltpu.VMEM)


def leave(x):
    return pltpu.with_memory_space_constraint(x, pltpu.HBM)


def distant_array(shape, dtype):
    return pltpu.HBM(shape, dtype)


def is_distant(shape):
    return getattr(shape, "memory_space", None) == pltpu.HBM


def factor_of(values):
    return lax.rsqrt(jnp.mean(values * values, axis=-1, keepdims=True) + 1e-06)


def head_into(hidden_ref, gain, out_ref):
    for i in range(0, ROWS, STEP):
        values = hidden_ref[i : i + STEP, :].astype(f32)
        out_ref[i : i + STEP, :] = (values * factor_of(values) * gain).astype(bf16)


def scores_of(queries, docs):
    dims = (((1,), (1,)), ((), ()))
    return FACTOR * lax.dot_general(queries, docs, dims, preferred_element_type=f32)


def across(column):
    return jnp.broadcast_to(column, (ROWS, LANES))


def onehot_of(positives_ref):
    slots = lax.broadcasted_iota(jnp.int32, (ROWS, ROWS), 0)
    return (slots == positives_ref[...]).astype(f32).T


def listed(neg_ref, distance):
    place, count = 0, 1
    for axis in AXES:
        place = place * lax.axis_size(axis) + lax.axis_index(axis)
        count = count * lax.axis_size(axis)
    sign = 1 - 2 * lax.rem(place, 2)
    block = lax.rem(place + sign * distance + count, count)
    found = neg_ref[0, 0] == block
    for i in range(1, neg_ref.shape[1]):
        found = jnp.logical_or(found, neg_ref[0, i] == block)
    return found


def doc_kernel(d_hbm, gain_hbm, dn_ref, gain_ref, d_ref, line_ref, sems):
    copies = [pltpu.make_async_copy(d_hbm, d_ref, sems.at[0]), pltpu.make_async_copy(gain_hbm, line_ref, sems.at[1])]
    for copy in copies:
        copy.start()
    for copy in copies:
        copy.wait()
    gain = jnp.concatenate([line_ref[i : i + 1, :] for i in range(GAIN_ROWS)], axis=1)
    gain_ref[...] = gain
    head_into(d_ref, gain, dn_ref)


def own_kernel(
    dn_ref, gain_ref, q_hbm, pos_hbm, qn_ref, s_ref, top_ref, total_ref, acc_ref, picked_ref, hot_ref, q_ref, pos_ref, sems
):
    copies = [pltpu.make_async_copy(q_hbm, q_ref, sems.at[0]), pltpu.make_async_copy(pos_hbm, pos_ref, sems.at[1])]
    for copy in copies:
        copy.start()
    for copy in copies:
        copy.wait()
    head_into(q_ref, gain_ref[...], qn_ref)
    scores = scores_of(qn_ref[...], dn_ref[...])
    top = jnp.max(scores, axis=1, keepdims=True)
    probs = jnp.exp(scores - top)
    s_ref[...] = scores
    top_ref[...] = across(top)
    total_ref[...] = across(jnp.sum(probs, axis=1, keepdims=True))
    probs = probs.astype(bf16)
    onehot = onehot_of(pos_ref)
    hot_ref[...] = onehot
    onehot = onehot.astype(bf16)
    for c in range(0, WIDTH, CHUNK):
        docs = dn_ref[:, c : c + CHUNK]
        acc_ref[:, c : c + CHUNK] = jnp.dot(probs, docs, preferred_element_type=f32)
        picked_ref[:, c : c + CHUNK] = jnp.dot(onehot, docs, preferred_element_type=f32).astype(bf16)


def head_kernel(x_ref, gain_ref, out_ref):
    head_into(x_ref, gain_ref[...], out_ref)


def fold(blocks, top0_ref, total0_ref):
    before = top0_ref[:, 0:1]
    top = before
    for scores in blocks:
        top = jnp.maximum(top, jnp.max(scores, axis=1, keepdims=True))
    shrink = jnp.exp(before - top)
    total = total0_ref[:, 0:1] * shrink
    probs = []
    for scores in blocks:
        prob = jnp.exp(scores - top)
        total = total + jnp.sum(prob, axis=1, keepdims=True)
        probs.append(prob.astype(bf16))
    return top, total, shrink, probs


def pair_kernel(
    distances, neg_ref, swap_ref, far_ref, qn_ref, top0_ref, total0_ref, acc0_ref,
    s_swap_ref, s_far_ref, top_ref, total_ref, acc_ref,
):
    for distance, dn_ref, s_ref in zip(distances, (swap_ref, far_ref), (s_swap_ref, s_far_ref)):
        s_ref[...] = jnp.where(listed(neg_ref, distance), scores_of(qn_ref[...], dn_ref[...]), HIDDEN)
    top, total, shrink, probs = fold((s_swap_ref[...], s_far_ref[...]), top0_ref, total0_ref)
    for c in range(0, WIDTH, CHUNK):
        cols = slice(c, c + CHUNK)
        term = jnp.dot(probs[0], swap_ref[:, cols], preferred_element_type=f32)
        term = term + jnp.dot(probs[1], far_ref[:, cols], preferred_element_type=f32)
        acc_ref[:, cols] = acc0_ref[:, cols] * shrink + term
    top_ref[...] = across(top)
    total_ref[...] = across(total)


def score_kernel(distance, neg_ref, dn_ref, qn_ref, s_ref):
    s_ref[...] = jnp.where(listed(neg_ref, distance), scores_of(qn_ref[...], dn_ref[...]), HIDDEN)


def last_kernel(
    distance, neg_ref, dn_ref, back_ref, s_back_ref, qn_ref, top0_ref, total0_ref, acc0_ref, picked_ref, s_own_ref,
    hot_ref, q_hbm, s_ref, lse_ref, gq_ref, lines, q_ref, sems,
):
    incoming = pltpu.make_async_copy(q_hbm, q_ref, sems.at[0])
    incoming.start()
    scores = jnp.where(listed(neg_ref, distance), scores_of(qn_ref[...], dn_ref[...]), HIDDEN)
    top, total, shrink, (probs, back_probs) = fold((scores, s_back_ref[...]), top0_ref, total0_ref)
    lse = top + jnp.log(total)
    s_ref[...] = scores
    lse_ref[...] = across(lse)
    incoming.wait()
    loss = jnp.sum(lse - jnp.sum(s_own_ref[...] * hot_ref[...], axis=1, keepdims=True))
    share = FACTOR / total
    kept_share = shrink * share
    squares = [
        jnp.sum(jnp.square(q_ref[i : i + STEP, :].astype(f32)), axis=-1, keepdims=True) for i in range(0, ROWS, STEP)
    ]
    factor = lax.rsqrt(jnp.concatenate(squares, axis=0) / WIDTH + 1e-06)
    for c in range(0, WIDTH, CHUNK):
        cols = slice(c, c + CHUNK)
        term = jnp.dot(probs, dn_ref[:, cols], preferred_element_type=f32)
        term = term + jnp.dot(back_probs, back_ref[:, cols], preferred_element_type=f32)
        gq = acc0_ref[:, cols] * kept_share + term * share - FACTOR * picked_ref[:, cols].astype(f32)
        gq_ref[:, cols] = gq
        added = 2.0 * jnp.sum(gq * (q_ref[:, cols].astype(f32) * factor), axis=0, keepdims=True)
        for i in range(0, CHUNK, LANES):
            lines[(c + i) // LANES : (c + i) // LANES + 1, :] = added[:, i : i + LANES]
    lines[GAIN_ROWS:, :] = jnp.full((SUM_ROWS - GAIN_ROWS, LANES), loss, f32)


def turned(block_ref, lse_ref, hot_ref=None):
    weight = jnp.exp(block_ref[...] - lse_ref[...])
    if hot_ref is not None:
        weight = weight - hot_ref[...]
    return weight.T.astype(bf16)


def near_kernel(qn_ref, lse_ref, s_relay_ref, s_swap_ref, s_back_ref, lines_ref, near_ref, back_ref, part_ref):
    w_relay, w_swap, w_back = (turned(block_ref, lse_ref) for block_ref in (s_relay_ref, s_swap_ref, s_back_ref))
    for c in range(0, WIDTH, CHUNK):
        cols = slice(c, c + CHUNK)
        queries = qn_ref[:, cols]
        near_ref[0, :, cols] = jnp.dot(w_relay, queries, preferred_element_type=f32).astype(bf16)
        near_ref[1, :, cols] = jnp.dot(w_swap, queries, preferred_element_type=f32).astype(bf16)
        back_ref[:, cols] = jnp.dot(w_back, queries, preferred_element_type=f32).astype(bf16)
    part_ref[...] = jnp.broadcast_to(lines_ref[...][None], part_ref.shape)


def far_kernel(qn_ref, lse_ref, s_far_ref, near_ref, far_ref):
    weight = turned(s_far_ref, lse_ref)
    for c in range(0, WIDTH, CHUNK):
        cols = slice(c, c + CHUNK)
        term = jnp.dot(weight, qn_ref[:, cols], preferred_element_type=f32)
        far_ref[:, cols] = (term + near_ref[0, :, cols].astype(f32)).astype(bf16)


def home_kernel(
    qn_ref, lse_ref, s_own_ref, hot_ref, near_ref, back_ref, gain_ref, gq_ref, q_hbm, own_ref, grad_hbm, q_ref, grad_ref, scaled_ref, sems
):
    incoming = pltpu.make_async_copy(q_hbm, q_ref, sems.at[PARTS])
    incoming.start()
    weight = turned(s_own_ref, lse_ref, hot_ref)
    for c in range(0, WIDTH, CHUNK):
        cols = slice(c, c + CHUNK)
        term = jnp.dot(weight, qn_ref[:, cols], preferred_element_type=f32)
        own_ref[:, cols] = term + near_ref[1, :, cols].astype(f32) + back_ref[:, cols].astype(f32)
    incoming.wait()

    def values_at(rows, cols):
        return q_ref[rows, cols].astype(f32)

    def cotangent_at(rows, cols):
        return gq_ref[rows, cols]

    send_parts(lambda rows: pull(values_at, cotangent_at, gain_ref, scaled_ref, grad_ref, rows), grad_ref, grad_hbm, sems)


def grad_doc_kernel(gain_ref, own_ref, far_ref, d_hbm, grad_hbm, d_ref, grad_ref, scaled_ref, sems, in_sems):
    incoming = []
    for part in range(PARTS):
        rows = pl.ds(part * PART, PART)
        copy = pltpu.make_async_copy(d_hbm.at[rows, :], d_ref.at[rows, :], in_sems.at[part])
        copy.start()
        incoming.append(copy)

    def values_at(rows, cols):
        return d_ref[rows, cols].astype(f32)

    def cotangent_at(rows, cols):
        return FACTOR * (own_ref[rows, cols] + far_ref[rows, cols].astype(f32))

    def work(rows):
        if rows.start % PART == 0:
            incoming[rows.start // PART].wait()
        pull(values_at, cotangent_at, gain_ref, scaled_ref, grad_ref, rows)

    send_parts(work, grad_ref, grad_hbm, sems)


def send_parts(work, out_ref, target, sems):
    outgoing = []
    for part in range(PARTS):
        for i in range(part * PART, (part + 1) * PART, STEP):
            work(slice(i, i + STEP))
        rows = pl.ds(part * PART, PART)
        copy = pltpu.make_async_copy(out_ref.at[rows, :], target.at[rows, :], sems.at[part])
        copy.start()
        outgoing.append(copy)
    for copy in outgoing:
        copy.wait()


def pull(values_at, cotangent_at, gain_ref, scaled_ref, out_ref, rows):
    square = jnp.zeros((STEP, CHUNK), f32)
    inner = jnp.zeros((STEP, CHUNK), f32)
    chunks = [slice(c, c + CHUNK) for c in range(0, WIDTH, CHUNK)]
    for cols in chunks:
        values = values_at(rows, cols)
        scaled = gain_ref[:, cols] * cotangent_at(rows, cols)
        scaled_ref[:, cols] = scaled
        square = square + values * values
        inner = inner + values * scaled
    factor = lax.rsqrt(jnp.sum(square, axis=-1, keepdims=True) / WIDTH + 1e-06)
    inner = factor * factor * factor * (jnp.sum(inner, axis=-1, keepdims=True) / WIDTH)
    for cols in chunks:
        grad = factor * scaled_ref[:, cols] - values_at(rows, cols) * inner
        out_ref[rows, cols] = grad.astype(bf16)


def sum_kernel(in_ref, out_ref):
    total = jnp.sum(in_ref[...], axis=0)
    out_ref[...] = jnp.broadcast_to(total[None], out_ref.shape)


def end_kernel(denom, in_ref, gain_ref, loss_ref):
    total = jnp.sum(in_ref[...], axis=0) / denom
    gain_ref[...] = total[:GAIN_ROWS]
    loss_ref[...] = total[GAIN_ROWS : GAIN_ROWS + 1, 0:1]


def body(query_hidden, doc_hidden, gain, positives, neg_blocks):
    count = lax.axis_size(AXES)
    gain = gain.reshape(GAIN_ROWS, LANES)
    positives = positives.reshape(1, ROWS)

    devices = range(count)
    far_source = [(i + 2 if i % 2 == 0 else i - 2) % count for i in devices]
    back_source = [(i - 2 if i % 2 == 0 else i + 2) % count for i in devices]

    def permute(x, route):
        return lax.ppermute(x, AXES, route)

    swap_route = [(i, i ^ 1) for i in devices]
    square, block = (ROWS, LANES), (ROWS, WIDTH)
    dma = pltpu.SemaphoreType.DMA
    far = permute(doc_hidden, [(far_source[i], i) for i in devices])
    dn, gain_line = call(
        doc_kernel,
        [held(block, bf16), held((1, WIDTH), f32)],
        (),
        distant=(leave(doc_hidden), leave(gain)),
        scratch=[pltpu.VMEM(block, bf16), pltpu.VMEM((GAIN_ROWS, LANES), f32), dma((2,))],
    )
    gain_line = kept(gain_line)
    back = permute(dn, [(back_source[i], i) for i in devices])
    swap = permute(dn, swap_route)
    qn, s_own, *state, picked, hot = call(
        own_kernel,
        [held(block, bf16)] + [held(square, f32)] * 3 + [held(block, f32), held(block, bf16), held(square, f32)],
        (kept(dn), gain_line),
        distant=(leave(query_hidden), leave(positives)),
        scratch=[pltpu.VMEM(block, bf16), pltpu.VMEM((1, ROWS), jnp.int32), dma((2,))],
    )
    qn, picked, s_own, hot = kept(qn), kept(picked), kept(s_own), kept(hot)
    far = call(head_kernel, held(block, bf16), (far, gain_line), after=(s_own,))
    relay = permute(far, swap_route)
    s_swap, s_far, *state = call(
        functools.partial(pair_kernel, (1, 2)),
        [held(square, f32)] * 4 + [held(block, f32)],
        (swap, far, qn, *map(kept, state)),
        scalars=(neg_blocks,),
        aliases={4: 2, 5: 3, 6: 4},
    )
    s_back = call(
        functools.partial(score_kernel, -2), held(square, f32), (back, qn), scalars=(neg_blocks,), after=(s_far,)
    )
    sizes = [lax.axis_size(a) for a in AXES]
    share = (SUM_ROWS, LANES)
    s_relay, lse, gq, lines = call(
        functools.partial(last_kernel, -1),
        [held(square, f32)] * 2 + [held(block, f32), held(share, f32)],
        (relay, back, kept(s_back), qn, *map(kept, state), picked, s_own, hot),
        scalars=(neg_blocks,),
        distant=(leave(query_hidden),),
        scratch=[pltpu.VMEM(block, bf16), dma((1,))],
        aliases={7: 2},
    )
    lse = kept(lse)

    def exchange(x, axis):
        return kept(lax.all_to_all(x, AXES[axis], 0, 0, tiled=True))

    def summed(x, axis, after=()):
        return call(sum_kernel, held((sizes[axis], *share), f32), (x,), after=after)

    t_near, t_back, part = call(
        near_kernel,
        [held((2, *block), bf16), held(block, bf16), held((sizes[0], *share), f32)],
        (qn, lse, kept(s_relay), kept(s_swap), kept(s_back), kept(lines)),
    )
    near_term = permute(t_near, swap_route)
    back_term = permute(t_back, [(i, back_source[i]) for i in devices])
    part = exchange(part, 0)
    far_sum = call(far_kernel, held(block, bf16), (qn, lse, kept(s_far), near_term), after=(part,))
    far_term = permute(far_sum, [(i, far_source[i]) for i in devices])
    t_own, grad_query = call(
        home_kernel,
        [held(block, f32), distant_array(block, bf16)],
        (qn, lse, s_own, hot, near_term, back_term, gain_line, kept(gq)),
        distant=(leave(query_hidden),),
        after=(far_sum,),
        scratch=[pltpu.VMEM(block, bf16), pltpu.VMEM(block, bf16), pltpu.VMEM((STEP, WIDTH), f32), dma((PARTS + 1,))],
    )
    part = summed(part, 1, after=(t_own,))
    part = summed(exchange(part, 1), 2)
    part = exchange(part, 2)
    grad_doc = call(
        grad_doc_kernel,
        distant_array(block, bf16),
        (gain_line, kept(t_own), far_term),
        distant=(leave(doc_hidden),),
        scratch=[
            pltpu.VMEM(block, bf16), pltpu.VMEM(block, bf16), pltpu.VMEM((STEP, WIDTH), f32), dma((PARTS,)), dma((PARTS,))
        ],
    )
    grad_gain, mean_loss = call(
        functools.partial(end_kernel, float(ROWS * count)),
        [jax.ShapeDtypeStruct((GAIN_ROWS, LANES), f32), jax.ShapeDtypeStruct((1, 1), f32)],
        (part,),
    )
    return mean_loss.reshape(()), grad_gain.reshape(WIDTH), grad_query, grad_doc


def grid_of(count):
    return (8, 12, 8) if count == 768 else (2, count // 16, 8)


def solution(mesh):
    devices = np.asarray(mesh.devices)
    inner = Mesh(devices.reshape(grid_of(devices.size)), AXES)
    placed = (P(AXES, None), P(AXES, None), P(), P(AXES), P(AXES, None))
    return jax.shard_map(
        body,
        mesh=inner,
        in_specs=placed,
        out_specs=(P(), P(), P(AXES, None), P(AXES, None)),
        check_vma=False,
    )
```

```python
import functools
import math

import jax
import jax.numpy as jnp
import numpy as np
from jax import lax
from jax.experimental import pallas as pl
from jax.experimental.pallas import tpu as pltpu
from jax.sharding import Mesh
from jax.sharding import PartitionSpec as P

logit_scale = 4.0
ROWS = 128
WIDTH = 3584
FACTOR = logit_scale / math.sqrt(WIDTH)
LANES = 128
GAIN_ROWS = WIDTH // LANES
SUM_ROWS = 32
CHUNK = 512
HIDDEN = -1e30
STEP = 16
PARTS = 4
PART = ROWS // PARTS
f32, bf16 = jnp.float32, jnp.bfloat16
AXES = ("y", "z", "row")

in_vmem = pl.BlockSpec(memory_space=pltpu.VMEM)
anywhere = pl.BlockSpec(memory_space=pl.ANY)
in_smem = pl.BlockSpec(memory_space=pltpu.SMEM)


def held(shape, dtype):
    return pltpu.VMEM(shape, dtype)


def call(kernel, out_shape, args, scratch=(), aliases=None, scalars=(), distant=(), after=(), flops=1000):
    given = len(scalars) + len(args) + len(distant)

    def run(*refs):
        kernel(*refs[:given], *refs[given + len(after) :])

    flat, tree = jax.tree.flatten(out_shape)
    outs = [anywhere if is_distant(x) else in_vmem for x in flat]
    return pl.pallas_call(
        run,
        in_specs=[in_smem] * len(scalars) + [in_vmem] * len(args) + [anywhere] * (len(distant) + len(after)),
        out_specs=jax.tree.unflatten(tree, outs),
        out_shape=out_shape,
        scratch_shapes=list(scratch),
        input_output_aliases=aliases or {},
        cost_estimate=pl.CostEstimate(flops=flops, bytes_accessed=1000, transcendentals=0),
        compiler_params=pltpu.CompilerParams(vmem_limit_bytes=15 * 2**20),
    )(*scalars, *args, *distant, *after)


def kept(x):
    return pltpu.with_memory_space_constraint(x, pltpu.VMEM)


def leave(x):
    return pltpu.with_memory_space_constraint(x, pltpu.HBM)


def distant_array(shape, dtype):
    return pltpu.HBM(shape, dtype)


def is_distant(shape):
    return getattr(shape, "memory_space", None) == pltpu.HBM


def factor_of(values):
    return lax.rsqrt(jnp.mean(values * values, axis=-1, keepdims=True) + 1e-06)


def head_into(hidden_ref, gain, out_ref):
    for i in range(0, ROWS, STEP):
        values = hidden_ref[i : i + STEP, :].astype(f32)
        out_ref[i : i + STEP, :] = (values * factor_of(values) * gain).astype(bf16)


def scores_of(queries, docs):
    dims = (((1,), (1,)), ((), ()))
    return FACTOR * lax.dot_general(queries, docs, dims, preferred_element_type=f32)


def across(column):
    return jnp.broadcast_to(column, (ROWS, LANES))


def onehot_of(positives_ref):
    slots = lax.broadcasted_iota(jnp.int32, (ROWS, ROWS), 0)
    return (slots == positives_ref[...]).astype(f32).T


def listed(neg_ref, distance):
    place, count = 0, 1
    for axis in AXES:
        place = place * lax.axis_size(axis) + lax.axis_index(axis)
        count = count * lax.axis_size(axis)
    sign = 1 - 2 * lax.rem(place, 2)
    block = lax.rem(place + sign * distance + count, count)
    found = neg_ref[0, 0] == block
    for i in range(1, neg_ref.shape[1]):
        found = jnp.logical_or(found, neg_ref[0, i] == block)
    return found


def doc_kernel(d_hbm, gain_hbm, dn_ref, gain_ref, d_ref, line_ref, sems):
    copies = [pltpu.make_async_copy(d_hbm, d_ref, sems.at[0]), pltpu.make_async_copy(gain_hbm, line_ref, sems.at[1])]
    for copy in copies:
        copy.start()
    for copy in copies:
        copy.wait()
    gain = jnp.concatenate([line_ref[i : i + 1, :] for i in range(GAIN_ROWS)], axis=1)
    gain_ref[...] = gain
    head_into(d_ref, gain, dn_ref)


def own_kernel(
    dn_ref, gain_ref, q_hbm, pos_hbm, qn_ref, s_ref, top_ref, total_ref, acc_ref, picked_ref, hot_ref, scaled_ref, q_ref, pos_ref, sems
):
    copies = [pltpu.make_async_copy(q_hbm, q_ref, sems.at[0]), pltpu.make_async_copy(pos_hbm, pos_ref, sems.at[1])]
    for copy in copies:
        copy.start()
    for copy in copies:
        copy.wait()
    gain = gain_ref[...]
    for i in range(0, ROWS, STEP):
        values = q_ref[i : i + STEP, :].astype(f32)
        scaled = values * factor_of(values)
        scaled_ref[i : i + STEP, :] = scaled
        qn_ref[i : i + STEP, :] = (scaled * gain).astype(bf16)
    scores = scores_of(qn_ref[...], dn_ref[...])
    top = jnp.max(scores, axis=1, keepdims=True)
    probs = jnp.exp(scores - top)
    s_ref[...] = scores
    top_ref[...] = across(top)
    total_ref[...] = across(jnp.sum(probs, axis=1, keepdims=True))
    probs = probs.astype(bf16)
    onehot = onehot_of(pos_ref)
    hot_ref[...] = onehot
    onehot = onehot.astype(bf16)
    for c in range(0, WIDTH, CHUNK):
        docs = dn_ref[:, c : c + CHUNK]
        acc_ref[:, c : c + CHUNK] = jnp.dot(probs, docs, preferred_element_type=f32)
        picked_ref[:, c : c + CHUNK] = jnp.dot(onehot, docs, preferred_element_type=f32).astype(bf16)


def head_kernel(x_ref, gain_ref, out_ref):
    head_into(x_ref, gain_ref[...], out_ref)


def fold(blocks, top0_ref, total0_ref):
    before = top0_ref[:, 0:1]
    top = before
    for scores in blocks:
        top = jnp.maximum(top, jnp.max(scores, axis=1, keepdims=True))
    shrink = jnp.exp(before - top)
    total = total0_ref[:, 0:1] * shrink
    probs = []
    for scores in blocks:
        prob = jnp.exp(scores - top)
        total = total + jnp.sum(prob, axis=1, keepdims=True)
        probs.append(prob.astype(bf16))
    return top, total, shrink, probs


def pair_kernel(
    distances, neg_ref, swap_ref, far_ref, qn_ref, top0_ref, total0_ref, acc0_ref,
    s_swap_ref, s_far_ref, top_ref, total_ref, acc_ref,
):
    for distance, dn_ref, s_ref in zip(distances, (swap_ref, far_ref), (s_swap_ref, s_far_ref)):
        s_ref[...] = jnp.where(listed(neg_ref, distance), scores_of(qn_ref[...], dn_ref[...]), HIDDEN)
    top, total, shrink, probs = fold((s_swap_ref[...], s_far_ref[...]), top0_ref, total0_ref)
    for c in range(0, WIDTH, CHUNK):
        cols = slice(c, c + CHUNK)
        term = jnp.dot(probs[0], swap_ref[:, cols], preferred_element_type=f32)
        term = term + jnp.dot(probs[1], far_ref[:, cols], preferred_element_type=f32)
        acc_ref[:, cols] = acc0_ref[:, cols] * shrink + term
    top_ref[...] = across(top)
    total_ref[...] = across(total)


def score_kernel(distance, neg_ref, dn_ref, qn_ref, s_ref):
    s_ref[...] = jnp.where(listed(neg_ref, distance), scores_of(qn_ref[...], dn_ref[...]), HIDDEN)


def last_kernel(
    distance, neg_ref, dn_ref, back_ref, s_back_ref, qn_ref, top0_ref, total0_ref, acc0_ref, picked_ref, s_own_ref,
    hot_ref, scaled_ref, s_ref, lse_ref, gq_ref, lines,
):
    scores = jnp.where(listed(neg_ref, distance), scores_of(qn_ref[...], dn_ref[...]), HIDDEN)
    top, total, shrink, (probs, back_probs) = fold((scores, s_back_ref[...]), top0_ref, total0_ref)
    lse = top + jnp.log(total)
    s_ref[...] = scores
    lse_ref[...] = across(lse)
    loss = jnp.sum(lse - jnp.sum(s_own_ref[...] * hot_ref[...], axis=1, keepdims=True))
    share = FACTOR / total
    kept_share = shrink * share
    for c in range(0, WIDTH, CHUNK):
        cols = slice(c, c + CHUNK)
        term = jnp.dot(probs, dn_ref[:, cols], preferred_element_type=f32)
        term = term + jnp.dot(back_probs, back_ref[:, cols], preferred_element_type=f32)
        gq = acc0_ref[:, cols] * kept_share + term * share - FACTOR * picked_ref[:, cols].astype(f32)
        gq_ref[:, cols] = gq
        added = 2.0 * jnp.sum(gq * scaled_ref[:, cols], axis=0, keepdims=True)
        for i in range(0, CHUNK, LANES):
            lines[(c + i) // LANES : (c + i) // LANES + 1, :] = added[:, i : i + LANES]
    lines[GAIN_ROWS:, :] = in_two(jnp.full((SUM_ROWS - GAIN_ROWS, LANES), loss, f32))


def in_two(value):
    head = value.astype(bf16).astype(f32)
    row = lax.broadcasted_iota(jnp.int32, value.shape, 0)
    return jnp.where(row == 0, head, jnp.where(row == 1, value - head, 0.0))


def turned(block_ref, lse_ref, hot_ref=None):
    weight = jnp.exp(block_ref[...] - lse_ref[...])
    if hot_ref is not None:
        weight = weight - hot_ref[...]
    return weight.T.astype(bf16)


def near_kernel(qn_ref, lse_ref, s_relay_ref, s_swap_ref, s_back_ref, lines_ref, near_ref, back_ref, part_ref):
    w_relay, w_swap, w_back = (turned(block_ref, lse_ref) for block_ref in (s_relay_ref, s_swap_ref, s_back_ref))
    for c in range(0, WIDTH, CHUNK):
        cols = slice(c, c + CHUNK)
        queries = qn_ref[:, cols]
        near_ref[0, :, cols] = jnp.dot(w_relay, queries, preferred_element_type=f32).astype(bf16)
        near_ref[1, :, cols] = jnp.dot(w_swap, queries, preferred_element_type=f32).astype(bf16)
        back_ref[:, cols] = jnp.dot(w_back, queries, preferred_element_type=f32).astype(bf16)
    part_ref[...] = jnp.broadcast_to(lines_ref[...].astype(bf16)[None], part_ref.shape)


def far_kernel(qn_ref, lse_ref, s_far_ref, near_ref, far_ref):
    weight = turned(s_far_ref, lse_ref)
    for c in range(0, WIDTH, CHUNK):
        cols = slice(c, c + CHUNK)
        term = jnp.dot(weight, qn_ref[:, cols], preferred_element_type=f32)
        far_ref[:, cols] = (term + near_ref[0, :, cols].astype(f32)).astype(bf16)


def home_kernel(
    qn_ref, lse_ref, s_own_ref, hot_ref, near_ref, back_ref, gain_ref, gq_ref, q_hbm, own_ref, grad_hbm, q_ref, grad_ref, scaled_ref, sems
):
    incoming = pltpu.make_async_copy(q_hbm, q_ref, sems.at[PARTS])
    incoming.start()
    weight = turned(s_own_ref, lse_ref, hot_ref)
    for c in range(0, WIDTH, CHUNK):
        cols = slice(c, c + CHUNK)
        term = jnp.dot(weight, qn_ref[:, cols], preferred_element_type=f32)
        own_ref[:, cols] = term + near_ref[1, :, cols].astype(f32) + back_ref[:, cols].astype(f32)
    incoming.wait()

    def values_at(rows, cols):
        return q_ref[rows, cols].astype(f32)

    def cotangent_at(rows, cols):
        return gq_ref[rows, cols]

    send_parts(lambda rows: pull(values_at, cotangent_at, gain_ref, scaled_ref, grad_ref, rows), grad_ref, grad_hbm, sems)


def grad_doc_kernel(gain_ref, own_ref, far_ref, d_hbm, grad_hbm, d_ref, grad_ref, scaled_ref, sems, in_sems):
    incoming = []
    for part in range(PARTS):
        rows = pl.ds(part * PART, PART)
        copy = pltpu.make_async_copy(d_hbm.at[rows, :], d_ref.at[rows, :], in_sems.at[part])
        copy.start()
        incoming.append(copy)

    def values_at(rows, cols):
        return d_ref[rows, cols].astype(f32)

    def cotangent_at(rows, cols):
        return FACTOR * (own_ref[rows, cols] + far_ref[rows, cols].astype(f32))

    def work(rows):
        if rows.start % PART == 0:
            incoming[rows.start // PART].wait()
        pull(values_at, cotangent_at, gain_ref, scaled_ref, grad_ref, rows)

    send_parts(work, grad_ref, grad_hbm, sems)


def send_parts(work, out_ref, target, sems):
    outgoing = []
    for part in range(PARTS):
        for i in range(part * PART, (part + 1) * PART, STEP):
            work(slice(i, i + STEP))
        rows = pl.ds(part * PART, PART)
        copy = pltpu.make_async_copy(out_ref.at[rows, :], target.at[rows, :], sems.at[part])
        copy.start()
        outgoing.append(copy)
    for copy in outgoing:
        copy.wait()


def pull(values_at, cotangent_at, gain_ref, scaled_ref, out_ref, rows):
    square = jnp.zeros((STEP, CHUNK), f32)
    inner = jnp.zeros((STEP, CHUNK), f32)
    chunks = [slice(c, c + CHUNK) for c in range(0, WIDTH, CHUNK)]
    for cols in chunks:
        values = values_at(rows, cols)
        scaled = gain_ref[:, cols] * cotangent_at(rows, cols)
        scaled_ref[:, cols] = scaled
        square = square + values * values
        inner = inner + values * scaled
    factor = lax.rsqrt(jnp.sum(square, axis=-1, keepdims=True) / WIDTH + 1e-06)
    inner = factor * factor * factor * (jnp.sum(inner, axis=-1, keepdims=True) / WIDTH)
    for cols in chunks:
        grad = factor * scaled_ref[:, cols] - values_at(rows, cols) * inner
        out_ref[rows, cols] = grad.astype(bf16)


def total_of(in_ref):
    total = jnp.sum(in_ref[...].astype(f32), axis=0)
    loss = total[GAIN_ROWS : GAIN_ROWS + 1] + total[GAIN_ROWS + 1 : GAIN_ROWS + 2]
    return total[:GAIN_ROWS], loss


def sum_kernel(in_ref, out_ref, lines):
    gain, loss = total_of(in_ref)
    lines[:GAIN_ROWS, :] = gain
    lines[GAIN_ROWS:, :] = in_two(jnp.broadcast_to(loss, (SUM_ROWS - GAIN_ROWS, LANES)))
    out_ref[...] = jnp.broadcast_to(lines[...].astype(bf16)[None], out_ref.shape)


def end_kernel(denom, in_ref, gain_ref, loss_ref):
    gain, loss = total_of(in_ref)
    gain_ref[...] = gain / denom
    loss_ref[...] = loss[:, 0:1] / denom


def body(query_hidden, doc_hidden, gain, positives, neg_blocks):
    count = lax.axis_size(AXES)
    gain = gain.reshape(GAIN_ROWS, LANES)
    positives = positives.reshape(1, ROWS)

    devices = range(count)
    far_source = [(i + 2 if i % 2 == 0 else i - 2) % count for i in devices]
    back_source = [(i - 2 if i % 2 == 0 else i + 2) % count for i in devices]

    def permute(x, route):
        return lax.ppermute(x, AXES, route)

    swap_route = [(i, i ^ 1) for i in devices]
    square, block = (ROWS, LANES), (ROWS, WIDTH)
    dma = pltpu.SemaphoreType.DMA
    far = permute(doc_hidden, [(far_source[i], i) for i in devices])
    dn, gain_line = call(
        doc_kernel,
        [held(block, bf16), held((1, WIDTH), f32)],
        (),
        distant=(leave(doc_hidden), leave(gain)),
        scratch=[pltpu.VMEM(block, bf16), pltpu.VMEM((GAIN_ROWS, LANES), f32), dma((2,))],
    )
    gain_line = kept(gain_line)
    back = permute(dn, [(back_source[i], i) for i in devices])
    swap = permute(dn, swap_route)
    qn, s_own, *state, picked, hot, scaled = call(
        own_kernel,
        [held(block, bf16)] + [held(square, f32)] * 3 + [held(block, f32), held(block, bf16), held(square, f32)]
        + [held(block, f32)],
        (kept(dn), gain_line),
        distant=(leave(query_hidden), leave(positives)),
        scratch=[pltpu.VMEM(block, bf16), pltpu.VMEM((1, ROWS), jnp.int32), dma((2,))],
    )
    qn, picked, s_own, hot = kept(qn), kept(picked), kept(s_own), kept(hot)
    far = call(head_kernel, held(block, bf16), (far, gain_line), after=(s_own,))
    relay = permute(far, swap_route)
    s_swap, s_far, *state = call(
        functools.partial(pair_kernel, (1, 2)),
        [held(square, f32)] * 4 + [held(block, f32)],
        (swap, far, qn, *map(kept, state)),
        scalars=(neg_blocks,),
        aliases={4: 2, 5: 3, 6: 4},
    )
    s_back = call(
        functools.partial(score_kernel, -2), held(square, f32), (back, qn), scalars=(neg_blocks,), after=(s_far,)
    )
    sizes = [lax.axis_size(a) for a in AXES]
    share = (SUM_ROWS, LANES)
    s_relay, lse, gq, lines = call(
        functools.partial(last_kernel, -1),
        [held(square, f32)] * 2 + [held(block, f32), held(share, f32)],
        (relay, back, kept(s_back), qn, *map(kept, state), picked, s_own, hot, kept(scaled)),
        scalars=(neg_blocks,),
        aliases={7: 2},
    )
    lse = kept(lse)

    def exchange(x, axis):
        return kept(lax.all_to_all(x, AXES[axis], 0, 0, tiled=True))

    def summed(x, axis, after=()):
        return call(
            sum_kernel, held((sizes[axis], *share), bf16), (x,), after=after, scratch=[pltpu.VMEM(share, f32)]
        )

    t_near, t_back, part = call(
        near_kernel,
        [held((2, *block), bf16), held(block, bf16), held((sizes[0], *share), bf16)],
        (qn, lse, kept(s_relay), kept(s_swap), kept(s_back), kept(lines)),
    )
    near_term = permute(t_near, swap_route)
    back_term = permute(t_back, [(i, back_source[i]) for i in devices])
    part = exchange(part, 0)
    far_sum = call(far_kernel, held(block, bf16), (qn, lse, kept(s_far), near_term), after=(part,))
    far_term = permute(far_sum, [(i, far_source[i]) for i in devices])
    t_own, grad_query = call(
        home_kernel,
        [held(block, f32), distant_array(block, bf16)],
        (qn, lse, s_own, hot, near_term, back_term, gain_line, kept(gq)),
        distant=(leave(query_hidden),),
        after=(far_sum,),
        scratch=[pltpu.VMEM(block, bf16), pltpu.VMEM(block, bf16), pltpu.VMEM((STEP, WIDTH), f32), dma((PARTS + 1,))],
    )
    part = summed(part, 1, after=(t_own,))
    ready = summed(exchange(part, 1), 2)
    part = exchange(ready, 2)
    grad_doc = call(
        grad_doc_kernel,
        distant_array(block, bf16),
        (gain_line, kept(t_own), far_term),
        distant=(leave(doc_hidden),),
        after=(ready,),
        scratch=[
            pltpu.VMEM(block, bf16), pltpu.VMEM(block, bf16), pltpu.VMEM((STEP, WIDTH), f32), dma((PARTS,)), dma((PARTS,))
        ],
        flops=3_000_000_000,
    )
    grad_gain, mean_loss = call(
        functools.partial(end_kernel, float(ROWS * count)),
        [jax.ShapeDtypeStruct((GAIN_ROWS, LANES), f32), jax.ShapeDtypeStruct((1, 1), f32)],
        (part,),
        after=(leave(grad_doc),),
    )
    return mean_loss.reshape(()), grad_gain.reshape(WIDTH), grad_query, grad_doc


def grid_of(count):
    return (8, 12, 8) if count == 768 else (2, count // 16, 8)


def solution(mesh):
    devices = np.asarray(mesh.devices)
    inner = Mesh(devices.reshape(grid_of(devices.size)), AXES)
    placed = (P(AXES, None), P(AXES, None), P(), P(AXES), P(AXES, None))
    return jax.shard_map(
        body,
        mesh=inner,
        in_specs=placed,
        out_specs=(P(), P(), P(AXES, None), P(AXES, None)),
        check_vma=False,
    )
```

```python
import functools
import math

import jax
import jax.numpy as jnp
import numpy as np
from jax import lax
from jax.experimental import pallas as pl
from jax.experimental.pallas import tpu as pltpu
from jax.sharding import Mesh
from jax.sharding import PartitionSpec as P

logit_scale = 4.0
ROWS = 128
WIDTH = 3584
FACTOR = logit_scale / math.sqrt(WIDTH)
LANES = 128
GAIN_ROWS = WIDTH // LANES
SUM_ROWS = 32
CHUNK = 512
HIDDEN = -1e30
STEP = 16
PARTS = 4
PART = ROWS // PARTS
f32, bf16 = jnp.float32, jnp.bfloat16
AXES = ("y", "z", "row")

in_vmem = pl.BlockSpec(memory_space=pltpu.VMEM)
anywhere = pl.BlockSpec(memory_space=pl.ANY)
in_smem = pl.BlockSpec(memory_space=pltpu.SMEM)


def held(shape, dtype):
    return pltpu.VMEM(shape, dtype)


def call(kernel, out_shape, args, scratch=(), aliases=None, scalars=(), distant=(), after=(), flops=1000):
    given = len(scalars) + len(args) + len(distant)

    def run(*refs):
        kernel(*refs[:given], *refs[given + len(after) :])

    flat, tree = jax.tree.flatten(out_shape)
    outs = [anywhere if is_distant(x) else in_vmem for x in flat]
    return pl.pallas_call(
        run,
        in_specs=[in_smem] * len(scalars) + [in_vmem] * len(args) + [anywhere] * (len(distant) + len(after)),
        out_specs=jax.tree.unflatten(tree, outs),
        out_shape=out_shape,
        scratch_shapes=list(scratch),
        input_output_aliases=aliases or {},
        cost_estimate=pl.CostEstimate(flops=flops, bytes_accessed=1000, transcendentals=0),
        compiler_params=pltpu.CompilerParams(vmem_limit_bytes=15 * 2**20),
    )(*scalars, *args, *distant, *after)


def kept(x):
    return pltpu.with_memory_space_constraint(x, pltpu.VMEM)


def leave(x):
    return pltpu.with_memory_space_constraint(x, pltpu.HBM)


def distant_array(shape, dtype):
    return pltpu.HBM(shape, dtype)


def is_distant(shape):
    return getattr(shape, "memory_space", None) == pltpu.HBM


def factor_of(values):
    return lax.rsqrt(jnp.mean(values * values, axis=-1, keepdims=True) + 1e-06)


def head_into(hidden_ref, gain, out_ref):
    for i in range(0, ROWS, STEP):
        values = hidden_ref[i : i + STEP, :].astype(f32)
        out_ref[i : i + STEP, :] = (values * factor_of(values) * gain).astype(bf16)


def scores_of(queries, docs):
    dims = (((1,), (1,)), ((), ()))
    return FACTOR * lax.dot_general(queries, docs, dims, preferred_element_type=f32)


def across(column):
    return jnp.broadcast_to(column, (ROWS, LANES))


def onehot_of(positives_ref):
    slots = lax.broadcasted_iota(jnp.int32, (ROWS, ROWS), 0)
    return (slots == positives_ref[...]).astype(f32).T


def listed(neg_ref, distance):
    place, count = 0, 1
    for axis in AXES:
        place = place * lax.axis_size(axis) + lax.axis_index(axis)
        count = count * lax.axis_size(axis)
    sign = 1 - 2 * lax.rem(place, 2)
    block = lax.rem(place + sign * distance + count, count)
    found = neg_ref[0, 0] == block
    for i in range(1, neg_ref.shape[1]):
        found = jnp.logical_or(found, neg_ref[0, i] == block)
    return found


def doc_kernel(d_hbm, gain_hbm, dn_ref, gain_ref, d_ref, line_ref, sems):
    copies = [pltpu.make_async_copy(d_hbm, d_ref, sems.at[0]), pltpu.make_async_copy(gain_hbm, line_ref, sems.at[1])]
    for copy in copies:
        copy.start()
    for copy in copies:
        copy.wait()
    gain = jnp.concatenate([line_ref[i : i + 1, :] for i in range(GAIN_ROWS)], axis=1)
    gain_ref[...] = gain
    head_into(d_ref, gain, dn_ref)


def own_kernel(
    dn_ref, gain_ref, q_hbm, pos_hbm, qn_ref, s_ref, top_ref, total_ref, acc_ref, picked_ref, hot_ref, scaled_ref, factor_ref, q_ref, pos_ref, sems
):
    copies = [pltpu.make_async_copy(q_hbm, q_ref, sems.at[0]), pltpu.make_async_copy(pos_hbm, pos_ref, sems.at[1])]
    for copy in copies:
        copy.start()
    for copy in copies:
        copy.wait()
    gain = gain_ref[...]
    for i in range(0, ROWS, STEP):
        values = q_ref[i : i + STEP, :].astype(f32)
        factor = factor_of(values)
        scaled = values * factor
        factor_ref[i : i + STEP, :] = jnp.broadcast_to(factor, (STEP, LANES))
        scaled_ref[i : i + STEP, :] = scaled
        qn_ref[i : i + STEP, :] = (scaled * gain).astype(bf16)
    scores = scores_of(qn_ref[...], dn_ref[...])
    top = jnp.max(scores, axis=1, keepdims=True)
    probs = jnp.exp(scores - top)
    s_ref[...] = scores
    top_ref[...] = across(top)
    total_ref[...] = across(jnp.sum(probs, axis=1, keepdims=True))
    probs = probs.astype(bf16)
    onehot = onehot_of(pos_ref)
    hot_ref[...] = onehot
    onehot = onehot.astype(bf16)
    for c in range(0, WIDTH, CHUNK):
        docs = dn_ref[:, c : c + CHUNK]
        acc_ref[:, c : c + CHUNK] = jnp.dot(probs, docs, preferred_element_type=f32)
        picked_ref[:, c : c + CHUNK] = jnp.dot(onehot, docs, preferred_element_type=f32).astype(bf16)


def head_kernel(x_ref, gain_ref, out_ref):
    head_into(x_ref, gain_ref[...], out_ref)


def fold(blocks, top0_ref, total0_ref):
    before = top0_ref[:, 0:1]
    top = before
    for scores in blocks:
        top = jnp.maximum(top, jnp.max(scores, axis=1, keepdims=True))
    shrink = jnp.exp(before - top)
    total = total0_ref[:, 0:1] * shrink
    probs = []
    for scores in blocks:
        prob = jnp.exp(scores - top)
        total = total + jnp.sum(prob, axis=1, keepdims=True)
        probs.append(prob.astype(bf16))
    return top, total, shrink, probs


def pair_kernel(
    distances, neg_ref, swap_ref, far_ref, qn_ref, top0_ref, total0_ref, acc0_ref,
    s_swap_ref, s_far_ref, top_ref, total_ref, acc_ref,
):
    for distance, dn_ref, s_ref in zip(distances, (swap_ref, far_ref), (s_swap_ref, s_far_ref)):
        s_ref[...] = jnp.where(listed(neg_ref, distance), scores_of(qn_ref[...], dn_ref[...]), HIDDEN)
    top, total, shrink, probs = fold((s_swap_ref[...], s_far_ref[...]), top0_ref, total0_ref)
    for c in range(0, WIDTH, CHUNK):
        cols = slice(c, c + CHUNK)
        term = jnp.dot(probs[0], swap_ref[:, cols], preferred_element_type=f32)
        term = term + jnp.dot(probs[1], far_ref[:, cols], preferred_element_type=f32)
        acc_ref[:, cols] = acc0_ref[:, cols] * shrink + term
    top_ref[...] = across(top)
    total_ref[...] = across(total)


def score_kernel(distance, neg_ref, dn_ref, qn_ref, s_ref):
    s_ref[...] = jnp.where(listed(neg_ref, distance), scores_of(qn_ref[...], dn_ref[...]), HIDDEN)


def last_kernel(
    distance, neg_ref, dn_ref, back_ref, s_back_ref, qn_ref, top0_ref, total0_ref, acc0_ref, picked_ref, s_own_ref,
    hot_ref, scaled_ref, s_ref, lse_ref, gq_ref, lines,
):
    scores = jnp.where(listed(neg_ref, distance), scores_of(qn_ref[...], dn_ref[...]), HIDDEN)
    top, total, shrink, (probs, back_probs) = fold((scores, s_back_ref[...]), top0_ref, total0_ref)
    lse = top + jnp.log(total)
    s_ref[...] = scores
    lse_ref[...] = across(lse)
    loss = jnp.sum(lse - jnp.sum(s_own_ref[...] * hot_ref[...], axis=1, keepdims=True))
    share = FACTOR / total
    kept_share = shrink * share
    for c in range(0, WIDTH, CHUNK):
        cols = slice(c, c + CHUNK)
        term = jnp.dot(probs, dn_ref[:, cols], preferred_element_type=f32)
        term = term + jnp.dot(back_probs, back_ref[:, cols], preferred_element_type=f32)
        gq = acc0_ref[:, cols] * kept_share + term * share - FACTOR * picked_ref[:, cols].astype(f32)
        gq_ref[:, cols] = gq
        added = 2.0 * jnp.sum(gq * scaled_ref[:, cols], axis=0, keepdims=True)
        for i in range(0, CHUNK, LANES):
            lines[(c + i) // LANES : (c + i) // LANES + 1, :] = added[:, i : i + LANES]
    lines[GAIN_ROWS:, :] = in_two(jnp.full((SUM_ROWS - GAIN_ROWS, LANES), loss, f32))


def in_two(value):
    head = value.astype(bf16).astype(f32)
    row = lax.broadcasted_iota(jnp.int32, value.shape, 0)
    return jnp.where(row == 0, head, jnp.where(row == 1, value - head, 0.0))


def turned(block_ref, lse_ref, hot_ref=None):
    weight = jnp.exp(block_ref[...] - lse_ref[...])
    if hot_ref is not None:
        weight = weight - hot_ref[...]
    return weight.T.astype(bf16)


def near_kernel(qn_ref, lse_ref, s_relay_ref, s_swap_ref, s_back_ref, lines_ref, near_ref, back_ref, part_ref):
    w_relay, w_swap, w_back = (turned(block_ref, lse_ref) for block_ref in (s_relay_ref, s_swap_ref, s_back_ref))
    for c in range(0, WIDTH, CHUNK):
        cols = slice(c, c + CHUNK)
        queries = qn_ref[:, cols]
        near_ref[0, :, cols] = jnp.dot(w_relay, queries, preferred_element_type=f32).astype(bf16)
        near_ref[1, :, cols] = jnp.dot(w_swap, queries, preferred_element_type=f32).astype(bf16)
        back_ref[:, cols] = jnp.dot(w_back, queries, preferred_element_type=f32).astype(bf16)
    part_ref[...] = jnp.broadcast_to(lines_ref[...].astype(bf16)[None], part_ref.shape)


def far_kernel(qn_ref, lse_ref, s_far_ref, near_ref, far_ref):
    weight = turned(s_far_ref, lse_ref)
    for c in range(0, WIDTH, CHUNK):
        cols = slice(c, c + CHUNK)
        term = jnp.dot(weight, qn_ref[:, cols], preferred_element_type=f32)
        far_ref[:, cols] = (term + near_ref[0, :, cols].astype(f32)).astype(bf16)


def home_kernel(
    qn_ref, lse_ref, s_own_ref, hot_ref, near_ref, back_ref, gain_ref, gq_ref, scaled_ref, factor_ref,
    own_ref, grad_hbm, grad_ref, sems,
):
    def work(rows):
        inner = jnp.zeros((STEP, CHUNK), f32)
        chunks = [slice(c, c + CHUNK) for c in range(0, WIDTH, CHUNK)]
        for cols in chunks:
            inner = inner + scaled_ref[rows, cols] * (gain_ref[:, cols] * gq_ref[rows, cols])
        inner = jnp.sum(inner, axis=-1, keepdims=True) / WIDTH
        factor = factor_ref[rows, 0:1]
        for cols in chunks:
            grad = gain_ref[:, cols] * gq_ref[rows, cols] - scaled_ref[rows, cols] * inner
            grad_ref[rows, cols] = (factor * grad).astype(bf16)

    def terms():
        weight = turned(s_own_ref, lse_ref, hot_ref)
        for c in range(0, WIDTH, CHUNK):
            cols = slice(c, c + CHUNK)
            term = jnp.dot(weight, qn_ref[:, cols], preferred_element_type=f32)
            own_ref[:, cols] = term + near_ref[1, :, cols].astype(f32) + back_ref[:, cols].astype(f32)

    send_parts(work, grad_ref, grad_hbm, sems, terms)


def grad_doc_kernel(gain_ref, own_ref, far_ref, d_hbm, grad_hbm, d_ref, grad_ref, scaled_ref, sems, in_sems):
    incoming = []
    for part in range(PARTS):
        rows = pl.ds(part * PART, PART)
        copy = pltpu.make_async_copy(d_hbm.at[rows, :], d_ref.at[rows, :], in_sems.at[part])
        copy.start()
        incoming.append(copy)

    def values_at(rows, cols):
        return d_ref[rows, cols].astype(f32)

    def cotangent_at(rows, cols):
        return FACTOR * (own_ref[rows, cols] + far_ref[rows, cols].astype(f32))

    def work(rows):
        if rows.start % PART == 0:
            incoming[rows.start // PART].wait()
        pull(values_at, cotangent_at, gain_ref, scaled_ref, grad_ref, rows)

    send_parts(work, grad_ref, grad_hbm, sems)


def send_parts(work, out_ref, target, sems, meanwhile=None):
    outgoing = []
    for part in range(PARTS):
        for i in range(part * PART, (part + 1) * PART, STEP):
            work(slice(i, i + STEP))
        rows = pl.ds(part * PART, PART)
        copy = pltpu.make_async_copy(out_ref.at[rows, :], target.at[rows, :], sems.at[part])
        copy.start()
        outgoing.append(copy)
    if meanwhile is not None:
        meanwhile()
    for copy in outgoing:
        copy.wait()


def pull(values_at, cotangent_at, gain_ref, scaled_ref, out_ref, rows):
    square = jnp.zeros((STEP, CHUNK), f32)
    inner = jnp.zeros((STEP, CHUNK), f32)
    chunks = [slice(c, c + CHUNK) for c in range(0, WIDTH, CHUNK)]
    for cols in chunks:
        values = values_at(rows, cols)
        scaled = gain_ref[:, cols] * cotangent_at(rows, cols)
        scaled_ref[:, cols] = scaled
        square = square + values * values
        inner = inner + values * scaled
    factor = lax.rsqrt(jnp.sum(square, axis=-1, keepdims=True) / WIDTH + 1e-06)
    inner = factor * factor * factor * (jnp.sum(inner, axis=-1, keepdims=True) / WIDTH)
    for cols in chunks:
        grad = factor * scaled_ref[:, cols] - values_at(rows, cols) * inner
        out_ref[rows, cols] = grad.astype(bf16)


def total_of(in_ref):
    total = jnp.sum(in_ref[...].astype(f32), axis=0)
    loss = total[GAIN_ROWS : GAIN_ROWS + 1] + total[GAIN_ROWS + 1 : GAIN_ROWS + 2]
    return total[:GAIN_ROWS], loss


def sum_kernel(in_ref, out_ref, lines):
    gain, loss = total_of(in_ref)
    lines[:GAIN_ROWS, :] = gain
    lines[GAIN_ROWS:, :] = in_two(jnp.broadcast_to(loss, (SUM_ROWS - GAIN_ROWS, LANES)))
    out_ref[...] = jnp.broadcast_to(lines[...].astype(bf16)[None], out_ref.shape)


def end_kernel(denom, in_ref, gain_ref, loss_ref):
    gain, loss = total_of(in_ref)
    gain_ref[...] = gain / denom
    loss_ref[...] = loss[:, 0:1] / denom


def body(query_hidden, doc_hidden, gain, positives, neg_blocks):
    count = lax.axis_size(AXES)
    gain = gain.reshape(GAIN_ROWS, LANES)
    positives = positives.reshape(1, ROWS)

    devices = range(count)
    far_source = [(i + 2 if i % 2 == 0 else i - 2) % count for i in devices]
    back_source = [(i - 2 if i % 2 == 0 else i + 2) % count for i in devices]

    def permute(x, route):
        return lax.ppermute(x, AXES, route)

    swap_route = [(i, i ^ 1) for i in devices]
    square, block = (ROWS, LANES), (ROWS, WIDTH)
    dma = pltpu.SemaphoreType.DMA
    far = permute(doc_hidden, [(far_source[i], i) for i in devices])
    dn, gain_line = call(
        doc_kernel,
        [held(block, bf16), held((1, WIDTH), f32)],
        (),
        distant=(leave(doc_hidden), leave(gain)),
        scratch=[pltpu.VMEM(block, bf16), pltpu.VMEM((GAIN_ROWS, LANES), f32), dma((2,))],
    )
    gain_line = kept(gain_line)
    back = permute(dn, [(back_source[i], i) for i in devices])
    swap = permute(dn, swap_route)
    qn, s_own, *state, picked, hot, scaled, factor = call(
        own_kernel,
        [held(block, bf16)] + [held(square, f32)] * 3 + [held(block, f32), held(block, bf16), held(square, f32)]
        + [held(block, f32), held(square, f32)],
        (kept(dn), gain_line),
        distant=(leave(query_hidden), leave(positives)),
        scratch=[pltpu.VMEM(block, bf16), pltpu.VMEM((1, ROWS), jnp.int32), dma((2,))],
    )
    qn, picked, s_own, hot = kept(qn), kept(picked), kept(s_own), kept(hot)
    far = call(head_kernel, held(block, bf16), (far, gain_line), after=(s_own,))
    relay = permute(far, swap_route)
    s_swap, s_far, *state = call(
        functools.partial(pair_kernel, (1, 2)),
        [held(square, f32)] * 4 + [held(block, f32)],
        (swap, far, qn, *map(kept, state)),
        scalars=(neg_blocks,),
        aliases={4: 2, 5: 3, 6: 4},
    )
    s_back = call(
        functools.partial(score_kernel, -2), held(square, f32), (back, qn), scalars=(neg_blocks,), after=(s_far,)
    )
    sizes = [lax.axis_size(a) for a in AXES]
    share = (SUM_ROWS, LANES)
    s_relay, lse, gq, lines = call(
        functools.partial(last_kernel, -1),
        [held(square, f32)] * 2 + [held(block, f32), held(share, f32)],
        (relay, back, kept(s_back), qn, *map(kept, state), picked, s_own, hot, kept(scaled)),
        scalars=(neg_blocks,),
        aliases={7: 2},
    )
    lse = kept(lse)

    def exchange(x, axis):
        return kept(lax.all_to_all(x, AXES[axis], 0, 0, tiled=True))

    def summed(x, axis, after=()):
        return call(
            sum_kernel, held((sizes[axis], *share), bf16), (x,), after=after, scratch=[pltpu.VMEM(share, f32)]
        )

    t_near, t_back, part = call(
        near_kernel,
        [held((2, *block), bf16), held(block, bf16), held((sizes[0], *share), bf16)],
        (qn, lse, kept(s_relay), kept(s_swap), kept(s_back), kept(lines)),
    )
    near_term = permute(t_near, swap_route)
    back_term = permute(t_back, [(i, back_source[i]) for i in devices])
    part = exchange(part, 0)
    far_sum = call(far_kernel, held(block, bf16), (qn, lse, kept(s_far), near_term), after=(part,))
    far_term = permute(far_sum, [(i, far_source[i]) for i in devices])
    t_own, grad_query = call(
        home_kernel,
        [held(block, f32), distant_array(block, bf16)],
        (qn, lse, s_own, hot, near_term, back_term, gain_line, kept(gq), kept(scaled), kept(factor)),
        after=(far_sum,),
        scratch=[pltpu.VMEM(block, bf16), dma((PARTS,))],
    )
    part = summed(part, 1, after=(t_own,))
    ready = summed(exchange(part, 1), 2)
    part = exchange(ready, 2)
    grad_doc = call(
        grad_doc_kernel,
        distant_array(block, bf16),
        (gain_line, kept(t_own), far_term),
        distant=(leave(doc_hidden),),
        after=(ready,),
        scratch=[
            pltpu.VMEM(block, bf16), pltpu.VMEM(block, bf16), pltpu.VMEM((STEP, WIDTH), f32), dma((PARTS,)), dma((PARTS,))
        ],
        flops=3_000_000_000,
    )
    grad_gain, mean_loss = call(
        functools.partial(end_kernel, float(ROWS * count)),
        [jax.ShapeDtypeStruct((GAIN_ROWS, LANES), f32), jax.ShapeDtypeStruct((1, 1), f32)],
        (part,),
        after=(leave(grad_doc),),
    )
    return mean_loss.reshape(()), grad_gain.reshape(WIDTH), grad_query, grad_doc


def grid_of(count):
    return (8, 12, 8) if count == 768 else (2, count // 16, 8)


def solution(mesh):
    devices = np.asarray(mesh.devices)
    inner = Mesh(devices.reshape(grid_of(devices.size)), AXES)
    placed = (P(AXES, None), P(AXES, None), P(), P(AXES), P(AXES, None))
    return jax.shard_map(
        body,
        mesh=inner,
        in_specs=placed,
        out_specs=(P(), P(), P(AXES, None), P(AXES, None)),
        check_vma=False,
    )
```

```python
import functools
import math

import jax
import jax.numpy as jnp
import numpy as np
from jax import lax
from jax.experimental import pallas as pl
from jax.experimental.pallas import tpu as pltpu
from jax.sharding import Mesh
from jax.sharding import PartitionSpec as P

logit_scale = 4.0
ROWS = 128
WIDTH = 3584
FACTOR = logit_scale / math.sqrt(WIDTH)
LANES = 128
GAIN_ROWS = WIDTH // LANES
SUM_ROWS = 32
CHUNK = 512
HIDDEN = -1e30
STEP = 16
PARTS = 4
PART = ROWS // PARTS
f32, bf16 = jnp.float32, jnp.bfloat16
AXES = ("y", "z", "row")

in_vmem = pl.BlockSpec(memory_space=pltpu.VMEM)
anywhere = pl.BlockSpec(memory_space=pl.ANY)
in_smem = pl.BlockSpec(memory_space=pltpu.SMEM)


def held(shape, dtype):
    return pltpu.VMEM(shape, dtype)


def call(kernel, out_shape, args, scratch=(), aliases=None, scalars=(), distant=(), after=(), flops=1000):
    given = len(scalars) + len(args) + len(distant)

    def run(*refs):
        kernel(*refs[:given], *refs[given + len(after) :])

    flat, tree = jax.tree.flatten(out_shape)
    outs = [anywhere if is_distant(x) else in_vmem for x in flat]
    return pl.pallas_call(
        run,
        in_specs=[in_smem] * len(scalars) + [in_vmem] * len(args) + [anywhere] * (len(distant) + len(after)),
        out_specs=jax.tree.unflatten(tree, outs),
        out_shape=out_shape,
        scratch_shapes=list(scratch),
        input_output_aliases=aliases or {},
        cost_estimate=pl.CostEstimate(flops=flops, bytes_accessed=1000, transcendentals=0),
        compiler_params=pltpu.CompilerParams(vmem_limit_bytes=15 * 2**20),
    )(*scalars, *args, *distant, *after)


def kept(x):
    return pltpu.with_memory_space_constraint(x, pltpu.VMEM)


def leave(x):
    return pltpu.with_memory_space_constraint(x, pltpu.HBM)


def distant_array(shape, dtype):
    return pltpu.HBM(shape, dtype)


def is_distant(shape):
    return getattr(shape, "memory_space", None) == pltpu.HBM


def factor_of(values):
    return lax.rsqrt(jnp.mean(values * values, axis=-1, keepdims=True) + 1e-06)


def head_into(hidden_ref, gain, out_ref):
    for i in range(0, ROWS, STEP):
        values = hidden_ref[i : i + STEP, :].astype(f32)
        out_ref[i : i + STEP, :] = (values * factor_of(values) * gain).astype(bf16)


def scores_of(queries, docs):
    dims = (((1,), (1,)), ((), ()))
    return FACTOR * lax.dot_general(queries, docs, dims, preferred_element_type=f32)


def across(column):
    return jnp.broadcast_to(column, (ROWS, LANES))


def onehot_of(positives_ref):
    slots = lax.broadcasted_iota(jnp.int32, (ROWS, ROWS), 0)
    return (slots == positives_ref[...]).astype(f32).T


def listed(neg_ref, distance):
    place, count = 0, 1
    for axis in AXES:
        place = place * lax.axis_size(axis) + lax.axis_index(axis)
        count = count * lax.axis_size(axis)
    sign = 1 - 2 * lax.rem(place, 2)
    block = lax.rem(place + sign * distance + count, count)
    found = neg_ref[0, 0] == block
    for i in range(1, neg_ref.shape[1]):
        found = jnp.logical_or(found, neg_ref[0, i] == block)
    return found


def doc_kernel(d_hbm, gain_hbm, dn_ref, gain_ref, d_ref, line_ref, sems):
    copies = [pltpu.make_async_copy(d_hbm, d_ref, sems.at[0]), pltpu.make_async_copy(gain_hbm, line_ref, sems.at[1])]
    for copy in copies:
        copy.start()
    for copy in copies:
        copy.wait()
    gain = jnp.concatenate([line_ref[i : i + 1, :] for i in range(GAIN_ROWS)], axis=1)
    gain_ref[...] = gain
    head_into(d_ref, gain, dn_ref)


def own_kernel(
    dn_ref, gain_ref, q_hbm, pos_hbm, qn_ref, s_ref, top_ref, total_ref, acc_ref, picked_ref, hot_ref, scaled_ref, factor_ref, q_ref, pos_ref, sems
):
    copies = [pltpu.make_async_copy(q_hbm, q_ref, sems.at[0]), pltpu.make_async_copy(pos_hbm, pos_ref, sems.at[1])]
    for copy in copies:
        copy.start()
    for copy in copies:
        copy.wait()
    gain = gain_ref[...]
    for i in range(0, ROWS, STEP):
        values = q_ref[i : i + STEP, :].astype(f32)
        factor = factor_of(values)
        scaled = values * factor
        factor_ref[i : i + STEP, :] = jnp.broadcast_to(factor, (STEP, LANES))
        scaled_ref[i : i + STEP, :] = scaled
        qn_ref[i : i + STEP, :] = (scaled * gain).astype(bf16)
    scores = scores_of(qn_ref[...], dn_ref[...])
    top = jnp.max(scores, axis=1, keepdims=True)
    probs = jnp.exp(scores - top)
    s_ref[...] = scores
    top_ref[...] = across(top)
    total_ref[...] = across(jnp.sum(probs, axis=1, keepdims=True))
    probs = probs.astype(bf16)
    onehot = onehot_of(pos_ref)
    hot_ref[...] = onehot
    onehot = onehot.astype(bf16)
    for c in range(0, WIDTH, CHUNK):
        docs = dn_ref[:, c : c + CHUNK]
        acc_ref[:, c : c + CHUNK] = jnp.dot(probs, docs, preferred_element_type=f32)
        picked_ref[:, c : c + CHUNK] = jnp.dot(onehot, docs, preferred_element_type=f32).astype(bf16)


def head_kernel(x_ref, gain_ref, out_ref):
    head_into(x_ref, gain_ref[...], out_ref)


def fold(blocks, top0_ref, total0_ref):
    before = top0_ref[:, 0:1]
    top = before
    for scores in blocks:
        top = jnp.maximum(top, jnp.max(scores, axis=1, keepdims=True))
    shrink = jnp.exp(before - top)
    total = total0_ref[:, 0:1] * shrink
    probs = []
    for scores in blocks:
        prob = jnp.exp(scores - top)
        total = total + jnp.sum(prob, axis=1, keepdims=True)
        probs.append(prob.astype(bf16))
    return top, total, shrink, probs


def pair_kernel(
    distances, neg_ref, swap_ref, far_ref, qn_ref, top0_ref, total0_ref, acc0_ref,
    s_swap_ref, s_far_ref, top_ref, total_ref, acc_ref,
):
    for distance, dn_ref, s_ref in zip(distances, (swap_ref, far_ref), (s_swap_ref, s_far_ref)):
        s_ref[...] = jnp.where(listed(neg_ref, distance), scores_of(qn_ref[...], dn_ref[...]), HIDDEN)
    top, total, shrink, probs = fold((s_swap_ref[...], s_far_ref[...]), top0_ref, total0_ref)
    for c in range(0, WIDTH, CHUNK):
        cols = slice(c, c + CHUNK)
        term = jnp.dot(probs[0], swap_ref[:, cols], preferred_element_type=f32)
        term = term + jnp.dot(probs[1], far_ref[:, cols], preferred_element_type=f32)
        acc_ref[:, cols] = acc0_ref[:, cols] * shrink + term
    top_ref[...] = across(top)
    total_ref[...] = across(total)


def score_kernel(distance, neg_ref, dn_ref, qn_ref, s_ref):
    s_ref[...] = jnp.where(listed(neg_ref, distance), scores_of(qn_ref[...], dn_ref[...]), HIDDEN)


def last_kernel(
    distance, neg_ref, dn_ref, back_ref, s_back_ref, qn_ref, top0_ref, total0_ref, acc0_ref, picked_ref, s_own_ref,
    hot_ref, scaled_ref, s_ref, lse_ref, gq_ref, lines,
):
    scores = jnp.where(listed(neg_ref, distance), scores_of(qn_ref[...], dn_ref[...]), HIDDEN)
    top, total, shrink, (probs, back_probs) = fold((scores, s_back_ref[...]), top0_ref, total0_ref)
    lse = top + jnp.log(total)
    s_ref[...] = scores
    lse_ref[...] = across(lse)
    loss = jnp.sum(lse - jnp.sum(s_own_ref[...] * hot_ref[...], axis=1, keepdims=True))
    share = FACTOR / total
    kept_share = shrink * share
    for c in range(0, WIDTH, CHUNK):
        cols = slice(c, c + CHUNK)
        term = jnp.dot(probs, dn_ref[:, cols], preferred_element_type=f32)
        term = term + jnp.dot(back_probs, back_ref[:, cols], preferred_element_type=f32)
        gq = acc0_ref[:, cols] * kept_share + term * share - FACTOR * picked_ref[:, cols].astype(f32)
        gq_ref[:, cols] = gq
        added = 2.0 * jnp.sum(gq * scaled_ref[:, cols], axis=0, keepdims=True)
        for i in range(0, CHUNK, LANES):
            lines[(c + i) // LANES : (c + i) // LANES + 1, :] = added[:, i : i + LANES]
    lines[GAIN_ROWS:, :] = in_two(jnp.full((SUM_ROWS - GAIN_ROWS, LANES), loss, f32))


def in_two(value):
    head = value.astype(bf16).astype(f32)
    row = lax.broadcasted_iota(jnp.int32, value.shape, 0)
    return jnp.where(row == 0, head, jnp.where(row == 1, value - head, 0.0))


def turned(block_ref, lse_ref, hot_ref=None):
    weight = jnp.exp(block_ref[...] - lse_ref[...])
    if hot_ref is not None:
        weight = weight - hot_ref[...]
    return weight.T.astype(bf16)


def near_kernel(qn_ref, lse_ref, s_relay_ref, s_swap_ref, s_back_ref, lines_ref, near_ref, back_ref, part_ref):
    w_relay, w_swap, w_back = (turned(block_ref, lse_ref) for block_ref in (s_relay_ref, s_swap_ref, s_back_ref))
    for c in range(0, WIDTH, CHUNK):
        cols = slice(c, c + CHUNK)
        queries = qn_ref[:, cols]
        near_ref[0, :, cols] = jnp.dot(w_relay, queries, preferred_element_type=f32).astype(bf16)
        near_ref[1, :, cols] = jnp.dot(w_swap, queries, preferred_element_type=f32).astype(bf16)
        back_ref[:, cols] = jnp.dot(w_back, queries, preferred_element_type=f32).astype(bf16)
    part_ref[...] = jnp.broadcast_to(lines_ref[...].astype(bf16)[None], part_ref.shape)


def far_kernel(qn_ref, lse_ref, s_far_ref, near_ref, far_ref):
    weight = turned(s_far_ref, lse_ref)
    for c in range(0, WIDTH, CHUNK):
        cols = slice(c, c + CHUNK)
        term = jnp.dot(weight, qn_ref[:, cols], preferred_element_type=f32)
        far_ref[:, cols] = (term + near_ref[0, :, cols].astype(f32)).astype(bf16)


def home_kernel(
    qn_ref, lse_ref, s_own_ref, hot_ref, near_ref, back_ref, gain_ref, gq_ref, scaled_ref, factor_ref,
    own_ref, grad_hbm, grad_ref, sems,
):
    def work(rows):
        inner = jnp.zeros((STEP, CHUNK), f32)
        chunks = [slice(c, c + CHUNK) for c in range(0, WIDTH, CHUNK)]
        for cols in chunks:
            inner = inner + scaled_ref[rows, cols] * (gain_ref[:, cols] * gq_ref[rows, cols])
        inner = jnp.sum(inner, axis=-1, keepdims=True) / WIDTH
        factor = factor_ref[rows, 0:1]
        for cols in chunks:
            grad = gain_ref[:, cols] * gq_ref[rows, cols] - scaled_ref[rows, cols] * inner
            grad_ref[rows, cols] = (factor * grad).astype(bf16)

    def terms():
        weight = turned(s_own_ref, lse_ref, hot_ref)
        for c in range(0, WIDTH, CHUNK):
            cols = slice(c, c + CHUNK)
            term = jnp.dot(weight, qn_ref[:, cols], preferred_element_type=f32)
            own_ref[:, cols] = term + near_ref[1, :, cols].astype(f32) + back_ref[:, cols].astype(f32)

    send_parts(work, grad_ref, grad_hbm, sems, terms)


def grad_doc_kernel(gain_ref, own_ref, far_hbm, d_hbm, grad_hbm, d_ref, far_ref, grad_ref, scaled_ref, sems, in_sems):
    incoming = []
    for part in range(PARTS):
        rows = pl.ds(part * PART, PART)
        for k, (source, target) in enumerate(((d_hbm, d_ref), (far_hbm, far_ref))):
            copy = pltpu.make_async_copy(source.at[rows, :], target.at[rows, :], in_sems.at[k, part])
            copy.start()
            incoming.append(copy)

    def values_at(rows, cols):
        return d_ref[rows, cols].astype(f32)

    def cotangent_at(rows, cols):
        return FACTOR * (own_ref[rows, cols] + far_ref[rows, cols].astype(f32))

    def work(rows):
        if rows.start % PART == 0:
            incoming[2 * (rows.start // PART)].wait()
            incoming[2 * (rows.start // PART) + 1].wait()
        pull(values_at, cotangent_at, gain_ref, scaled_ref, grad_ref, rows)

    send_parts(work, grad_ref, grad_hbm, sems)


def send_parts(work, out_ref, target, sems, meanwhile=None):
    outgoing = []
    for part in range(PARTS):
        for i in range(part * PART, (part + 1) * PART, STEP):
            work(slice(i, i + STEP))
        rows = pl.ds(part * PART, PART)
        copy = pltpu.make_async_copy(out_ref.at[rows, :], target.at[rows, :], sems.at[part])
        copy.start()
        outgoing.append(copy)
    if meanwhile is not None:
        meanwhile()
    for copy in outgoing:
        copy.wait()


def pull(values_at, cotangent_at, gain_ref, scaled_ref, out_ref, rows):
    square = jnp.zeros((STEP, CHUNK), f32)
    inner = jnp.zeros((STEP, CHUNK), f32)
    chunks = [slice(c, c + CHUNK) for c in range(0, WIDTH, CHUNK)]
    for cols in chunks:
        values = values_at(rows, cols)
        scaled = gain_ref[:, cols] * cotangent_at(rows, cols)
        scaled_ref[:, cols] = scaled
        square = square + values * values
        inner = inner + values * scaled
    factor = lax.rsqrt(jnp.sum(square, axis=-1, keepdims=True) / WIDTH + 1e-06)
    inner = factor * factor * factor * (jnp.sum(inner, axis=-1, keepdims=True) / WIDTH)
    for cols in chunks:
        grad = factor * scaled_ref[:, cols] - values_at(rows, cols) * inner
        out_ref[rows, cols] = grad.astype(bf16)


def total_of(in_ref):
    total = jnp.sum(in_ref[...].astype(f32), axis=0)
    loss = total[GAIN_ROWS : GAIN_ROWS + 1] + total[GAIN_ROWS + 1 : GAIN_ROWS + 2]
    return total[:GAIN_ROWS], loss


def sum_kernel(in_ref, out_ref, lines):
    gain, loss = total_of(in_ref)
    lines[:GAIN_ROWS, :] = gain
    lines[GAIN_ROWS:, :] = in_two(jnp.broadcast_to(loss, (SUM_ROWS - GAIN_ROWS, LANES)))
    out_ref[...] = jnp.broadcast_to(lines[...].astype(bf16)[None], out_ref.shape)


def end_kernel(denom, in_ref, gain_ref, loss_ref):
    gain, loss = total_of(in_ref)
    gain_ref[...] = gain / denom
    loss_ref[...] = loss[:, 0:1] / denom


def body(query_hidden, doc_hidden, gain, positives, neg_blocks):
    count = lax.axis_size(AXES)
    gain = gain.reshape(GAIN_ROWS, LANES)
    positives = positives.reshape(1, ROWS)

    devices = range(count)
    far_source = [(i + 2 if i % 2 == 0 else i - 2) % count for i in devices]
    back_source = [(i - 2 if i % 2 == 0 else i + 2) % count for i in devices]

    def permute(x, route):
        return lax.ppermute(x, AXES, route)

    swap_route = [(i, i ^ 1) for i in devices]
    square, block = (ROWS, LANES), (ROWS, WIDTH)
    dma = pltpu.SemaphoreType.DMA
    far = permute(doc_hidden, [(far_source[i], i) for i in devices])
    dn, gain_line = call(
        doc_kernel,
        [held(block, bf16), held((1, WIDTH), f32)],
        (),
        distant=(leave(doc_hidden), leave(gain)),
        scratch=[pltpu.VMEM(block, bf16), pltpu.VMEM((GAIN_ROWS, LANES), f32), dma((2,))],
    )
    gain_line = kept(gain_line)
    back = permute(dn, [(back_source[i], i) for i in devices])
    swap = permute(dn, swap_route)
    qn, s_own, *state, picked, hot, scaled, factor = call(
        own_kernel,
        [held(block, bf16)] + [held(square, f32)] * 3 + [held(block, f32), held(block, bf16), held(square, f32)]
        + [held(block, f32), held(square, f32)],
        (kept(dn), gain_line),
        distant=(leave(query_hidden), leave(positives)),
        scratch=[pltpu.VMEM(block, bf16), pltpu.VMEM((1, ROWS), jnp.int32), dma((2,))],
    )
    qn, picked, s_own, hot = kept(qn), kept(picked), kept(s_own), kept(hot)
    far = call(head_kernel, held(block, bf16), (far, gain_line), after=(s_own,))
    relay = permute(far, swap_route)
    s_swap, s_far, *state = call(
        functools.partial(pair_kernel, (1, 2)),
        [held(square, f32)] * 4 + [held(block, f32)],
        (swap, far, qn, *map(kept, state)),
        scalars=(neg_blocks,),
        aliases={4: 2, 5: 3, 6: 4},
    )
    s_back = call(
        functools.partial(score_kernel, -2), held(square, f32), (back, qn), scalars=(neg_blocks,), after=(s_far,)
    )
    sizes = [lax.axis_size(a) for a in AXES]
    share = (SUM_ROWS, LANES)
    s_relay, lse, gq, lines = call(
        functools.partial(last_kernel, -1),
        [held(square, f32)] * 2 + [held(block, f32), held(share, f32)],
        (relay, back, kept(s_back), qn, *map(kept, state), picked, s_own, hot, kept(scaled)),
        scalars=(neg_blocks,),
        aliases={7: 2},
    )
    lse = kept(lse)

    def exchange(x, axis):
        return kept(lax.all_to_all(x, AXES[axis], 0, 0, tiled=True))

    def summed(x, axis, after=()):
        return call(
            sum_kernel, held((sizes[axis], *share), bf16), (x,), after=after, scratch=[pltpu.VMEM(share, f32)]
        )

    t_near, t_back, part = call(
        near_kernel,
        [held((2, *block), bf16), held(block, bf16), held((sizes[0], *share), bf16)],
        (qn, lse, kept(s_relay), kept(s_swap), kept(s_back), kept(lines)),
    )
    near_term = permute(t_near, swap_route)
    back_term = permute(t_back, [(i, back_source[i]) for i in devices])
    part = exchange(part, 0)
    far_sum = call(far_kernel, held(block, bf16), (qn, lse, kept(s_far), near_term), after=(part,))
    far_term = permute(far_sum, [(i, far_source[i]) for i in devices])
    t_own, grad_query = call(
        home_kernel,
        [held(block, f32), distant_array(block, bf16)],
        (qn, lse, s_own, hot, near_term, back_term, gain_line, kept(gq), kept(scaled), kept(factor)),
        after=(far_sum,),
        scratch=[pltpu.VMEM(block, bf16), dma((PARTS,))],
    )
    part = summed(part, 1, after=(t_own,))
    ready = summed(exchange(part, 1), 2)
    part = exchange(ready, 2)
    grad_doc = call(
        grad_doc_kernel,
        distant_array(block, bf16),
        (gain_line, kept(t_own)),
        distant=(far_term, leave(doc_hidden)),
        after=(ready,),
        scratch=[
            pltpu.VMEM(block, bf16), pltpu.VMEM(block, bf16), pltpu.VMEM(block, bf16), pltpu.VMEM((STEP, WIDTH), f32),
            dma((PARTS,)), dma((2, PARTS)),
        ],
        flops=3_000_000_000,
    )
    grad_gain, mean_loss = call(
        functools.partial(end_kernel, float(ROWS * count)),
        [jax.ShapeDtypeStruct((GAIN_ROWS, LANES), f32), jax.ShapeDtypeStruct((1, 1), f32)],
        (part,),
        after=(leave(grad_doc),),
    )
    return mean_loss.reshape(()), grad_gain.reshape(WIDTH), grad_query, grad_doc


def grid_of(count):
    return (8, 12, 8) if count == 768 else (2, count // 16, 8)


def solution(mesh):
    devices = np.asarray(mesh.devices)
    inner = Mesh(devices.reshape(grid_of(devices.size)), AXES)
    placed = (P(AXES, None), P(AXES, None), P(), P(AXES), P(AXES, None))
    return jax.shard_map(
        body,
        mesh=inner,
        in_specs=placed,
        out_specs=(P(), P(), P(AXES, None), P(AXES, None)),
        check_vma=False,
    )
```
